256 devices in a mesh: seq: 32 (over y, z_lo, core), mp: 8 (over x, z_hi).
Axes of the slice: x: 4, y: 4, z: 8 (z_hi: 2, z_lo: 4; z = z_hi * 4 + z_lo), core: 2. Of those that a mesh axis runs over, the one named last changes fastest.
Arguments:
- query: bfloat16 [24576, 4096], P('seq', 'mp'), may hold values from -5 to 5
- key: bfloat16 [24576, 4096], P('seq', 'mp'), may hold values from -5 to 5
- value: bfloat16 [24576, 4096], P('seq', 'mp'), may hold values from -6 to 6
- weight_out: bfloat16 [4096, 4096], P('mp', 'seq'), may hold values from -0.09375 to 0.09375
- output_gradient: bfloat16 [24576, 4096], P('seq', 'mp'), may hold values from -6 to 6
Outputs:
- output: bfloat16 [24576, 4096], P('seq', 'mp')
- grad_query: bfloat16 [24576, 4096], P('seq', 'mp')
- grad_key: bfloat16 [24576, 4096], P('seq', 'mp')
- grad_value: bfloat16 [24576, 4096], P('seq', 'mp')
- grad_weight: bfloat16 [4096, 4096], P('mp', 'seq')
The draws below stay inside these ranges and needn't reach their ends.
All inputs are finite; a program needn't handle non-finite values.
Results may differ from the reference program's by a relative error of at most 0.03.
Values may be sent and summed in bfloat16 or wider, within the bound.
A program may use at most 128 MiB of HBM per device.

```python
import jax
import jax.numpy as jnp
from jax import lax

HEAD_WIDTH = 128
HEADS_DEV = 4
ROW_LENGTH = 256
HEAD_TOTAL = 32
ROW_TOTAL = 96
N_MP = 8


def draw_query(key, part):
    key = jax.random.fold_in(key, 1)
    base_offset = jax.random.truncated_normal(key, -5.0, 5.0, (ROW_TOTAL * ROW_LENGTH, HEAD_TOTAL * HEAD_WIDTH), jnp.float32)
    return base_offset.astype(jnp.bfloat16)


def draw_key(key, part):
    key = jax.random.fold_in(key, 2)
    base_offset = jax.random.truncated_normal(key, -5.0, 5.0, (ROW_TOTAL * ROW_LENGTH, HEAD_TOTAL * HEAD_WIDTH), jnp.float32)
    return base_offset.astype(jnp.bfloat16)


def spiked(array, stream_key, source, target, parts, factor):
    owner, partner = [(jnp.arange(array.shape[axis_at]) // (array.shape[axis_at] // parts)).reshape([-1 if axis == axis_at else 1 for axis in range(array.ndim)]) for axis_at in (source, target)]
    chosen = jax.random.permutation(stream_key, parts)[partner]
    strong = (owner == chosen) | (owner == (partner + parts // 2) % parts)
    return jnp.where(strong, factor * array, array)


def block_levels(rng, dims, pieces, low, top_value):
    level = 1.0
    for dim, blocks in pieces:
        heights = jax.random.uniform(jax.random.fold_in(jax.random.fold_in(rng, 6), dim), (blocks,), jnp.float32, low / len(pieces), top_value / len(pieces))
        level = level * jnp.repeat(jnp.exp(heights), dims[dim] // blocks).reshape((-1,) + (1,) * (len(dims) - 1 - dim))
    return level


def bell_draw(rng, extent, spread, reach, pieces=(), dtype=jnp.bfloat16):
    entries = spread * jax.random.normal(rng, extent, jnp.float32)
    if pieces:
        entries = entries * block_levels(rng, extent, pieces, -0.22, 0.18)
    return jnp.clip(entries, -reach, reach).astype(dtype)


def gaussian_with(rng, extent, scale, limit, pieces, heavy, kind=jnp.bfloat16):
    entries = scale * jax.random.normal(rng, extent, jnp.float32)
    if pieces:
        entries = entries * block_levels(rng, extent, pieces, -0.22, 0.18)
    return jnp.clip(spiked(entries, jax.random.fold_in(rng, 3), *heavy), -limit, limit).astype(kind)


def setup_inputs(seed: int = 0) -> dict:
    splits = jax.random.split(jax.random.key(seed), 6)
    return {
        "query": draw_query(jax.random.fold_in(splits[5], 71), 0),
        "key": draw_key(jax.random.fold_in(splits[5], 71), 0),
        "value": bell_draw(splits[2], (ROW_TOTAL * ROW_LENGTH, HEAD_TOTAL * HEAD_WIDTH), 1.0, 6.0, ((0, 32), (1, 8))),
        "weight_out": bell_draw(splits[3], (HEAD_TOTAL * HEAD_WIDTH, HEAD_TOTAL * HEAD_WIDTH), (HEAD_TOTAL * HEAD_WIDTH) ** -0.5, 0.09375, ((0, 8), (1, 32))),
        "output_gradient": gaussian_with(splits[4], (ROW_TOTAL * ROW_LENGTH, HEAD_TOTAL * HEAD_WIDTH), 1.0, 6.0, ((0, 32), (1, 8)), (0, 1, 32, 2.75)),
    }


def attend(queries, keys, values, grad_out, permitted_mask, factor):
    wide_keys = keys.astype(jnp.float32)
    wide_queries = queries.astype(jnp.float32)
    wide_values = values.astype(jnp.float32)
    scores = jnp.einsum("bqhe,bkhe->bhqk", wide_queries, wide_keys) * factor
    scores = jnp.where(permitted_mask, scores, -1e30)
    highest = jnp.max(scores, axis=-1, keepdims=True)
    weights = jnp.exp(scores - highest)
    probs = lax.optimization_barrier((weights / jnp.sum(weights, axis=-1, keepdims=True)).astype(jnp.bfloat16))
    probs_wide = probs.astype(jnp.float32)
    outputs = lax.optimization_barrier(jnp.einsum("bhqk,bkhe->bqhe", probs_wide, wide_values).astype(jnp.bfloat16))
    grad_wide = grad_out.astype(jnp.float32)
    grad_probs = jnp.einsum("bqhe,bkhe->bhqk", grad_wide, wide_values)
    centre = jnp.einsum("bqhe,bqhe->bhq", grad_wide, outputs.astype(jnp.float32))[..., None]
    grad_scores = lax.optimization_barrier((probs_wide * (grad_probs - centre)).astype(jnp.bfloat16)).astype(jnp.float32)
    grad_queries = jnp.einsum("bhqk,bkhe->bqhe", grad_scores, wide_keys) * factor
    grad_keys = jnp.einsum("bhqk,bqhe->bkhe", grad_scores, wide_queries) * factor
    grad_values = jnp.einsum("bhqk,bqhe->bkhe", probs_wide, grad_wide)
    return outputs, grad_queries, grad_keys, grad_values


def reference(query, key, value, weight_out, output_gradient):
    grand_total = ROW_TOTAL * ROW_LENGTH
    half_width = HEADS_DEV // 2
    factor = HEAD_WIDTH ** -0.5
    share = HEADS_DEV * HEAD_WIDTH
    width = HEAD_TOTAL * HEAD_WIDTH
    grad_mixed = jnp.dot(output_gradient, weight_out.T, preferred_element_type=jnp.float32).astype(jnp.bfloat16)

    def split(input_tensor):
        position_lattice = input_tensor.reshape(grand_total, N_MP, HEADS_DEV, HEAD_WIDTH)
        row_portion = position_lattice[:, :, :half_width].reshape(ROW_TOTAL, ROW_LENGTH, N_MP * half_width, HEAD_WIDTH)
        column_portion = position_lattice[:, :, half_width:].reshape(ROW_TOTAL, ROW_LENGTH, N_MP * half_width, HEAD_WIDTH)
        return row_portion, column_portion

    def columns(input_tensor):
        return jnp.transpose(input_tensor, (1, 0, 2, 3))

    def previous(rows):
        return jnp.concatenate([jnp.zeros_like(rows[:1]), rows[:-1]], axis=0)

    row_query, col_query = split(query)
    row_key, col_key = split(key)
    row_value, col_value = split(value)
    row_grad, col_grad = split(grad_mixed)
    row_keys = jnp.concatenate([previous(row_key), row_key], axis=1)
    row_values = jnp.concatenate([previous(row_value), row_value], axis=1)
    token_position = jnp.arange(ROW_LENGTH)[:, None]
    target_index = jnp.arange(2 * ROW_LENGTH)[None, :]
    attention_window = (target_index > token_position) & (target_index <= token_position + ROW_LENGTH)
    openings = jnp.arange(ROW_TOTAL) == 0

    def per_row(inputs):
        queries, keys, values, grads, initial_window = inputs
        permitted_mask = attention_window & ((target_index >= ROW_LENGTH) | jnp.logical_not(initial_window))
        results = attend(queries[None], keys[None], values[None], grads[None], permitted_mask[None, None], factor)
        return tuple(part[0] for part in results)

    row_out, row_gquery, row_key_gradient, row_value_gradient = lax.map(per_row, (row_query, row_keys, row_values, row_grad, openings))

    def settle(value_portion):
        subsequent_rows = jnp.concatenate([value_portion[1:, :ROW_LENGTH], jnp.zeros_like(value_portion[:1, :ROW_LENGTH])], axis=0)
        return (value_portion[:, ROW_LENGTH:] + subsequent_rows).astype(jnp.bfloat16)

    causal = jnp.arange(ROW_TOTAL)[:, None] >= jnp.arange(ROW_TOTAL)[None, :]
    col_out, col_gquery, col_gkey, col_gvalue = attend(columns(col_query), columns(col_key), columns(col_value), columns(col_grad), causal[None, None], factor)

    def join(row_portion, column_portion):
        left = row_portion.reshape(grand_total, N_MP, half_width, HEAD_WIDTH)
        right = columns(column_portion).reshape(grand_total, N_MP, half_width, HEAD_WIDTH)
        return jnp.concatenate([left, right], axis=2).reshape(grand_total, width)

    mixed = join(row_out, col_out)
    grad_query = join(row_gquery.astype(jnp.bfloat16), col_gquery.astype(jnp.bfloat16))
    grad_key = join(settle(row_key_gradient), col_gkey.astype(jnp.bfloat16))
    grad_value = join(settle(row_value_gradient), col_gvalue.astype(jnp.bfloat16))
    summed = jnp.zeros((grand_total, width), jnp.float32)
    for group in range(N_MP):
        value_portion = jnp.dot(mixed[:, group * share:(group + 1) * share], weight_out[group * share:(group + 1) * share], preferred_element_type=jnp.float32)
        summed = summed + lax.optimization_barrier(value_portion.astype(jnp.bfloat16)).astype(jnp.float32)
    grad_weight = jnp.dot(mixed.T, output_gradient, preferred_element_type=jnp.float32).astype(jnp.bfloat16)
    return (summed.astype(jnp.bfloat16), grad_query, grad_key, grad_value, grad_weight)
```

```python
import jax
import jax.numpy as jnp
from jax import lax
from jax.experimental import pallas as pl
from jax.experimental.pallas import tpu as pltpu
from jax.sharding import PartitionSpec as P

HEAD_WIDTH = 128
ROW_LENGTH = 256
MESH = pl.DeviceIdType.MESH
F32 = jnp.float32
BF16 = jnp.bfloat16


def coords():
    s = lax.axis_index("seq")
    m = lax.axis_index("mp")
    return s // 8, (s // 2) % 4, s % 2, m // 2, m % 2


def device(y, zl, c, x, zh):
    return (y * 8 + zl * 2 + c, x * 2 + zh)


def remote(src, dst, send, recv, target):
    return pltpu.make_async_remote_copy(
        src_ref=src, dst_ref=dst, send_sem=send, recv_sem=recv, device_id=target, device_id_type=MESH
    )


def arrive(ref, sem):
    pltpu.make_async_copy(ref, ref, sem).wait()


def greet(targets):
    barrier = pltpu.get_barrier_semaphore()
    for target in targets:
        pl.semaphore_signal(barrier, inc=1, device_id=target, device_id_type=MESH)
    pl.semaphore_wait(barrier, len(targets))


def neighbours():
    y, zl, c, x, zh = coords()
    core = device(y, zl, 1 - c, x, zh)
    lines = [device(y, (zl + d) % 4, c, x, zh) for d in (1, 2, 3)]
    rings = [device((y + d) % 4, zl, c, x, zh) for d in (1, 2, 3)]
    right = device(y, zl, c, (x + 1) % 4, zh)
    left = device(y, zl, c, (x + 3) % 4, zh)
    far = device(y, zl, c, x, 1 - zh)
    return core, lines, rings, right, left, far


def wide(index, width):
    return pl.ds(pl.multiple_of(index * width, width), width)


def gather_kernel(
    w_ref, og_ref, w_out, og_out, gm_ref, w_buf, og_buf, own_sem, w_send, w_recv, o_send, o_recv, out_sem
):
    y, zl, c, x, zh = coords()
    core, lines, rings, right, left, far = neighbours()
    greet([core, *lines, *rings, right, left, far])

    def w_at(yy, zz, cc):
        return w_buf.at[:, wide(yy * 8 + zz * 2 + cc, 128)]

    def og_at(xx, hh):
        return og_buf.at[:, wide(xx * 2 + hh, 512)]

    def og_half(xx, hh, half):
        return og_buf.at[pl.ds(384 * half, 384), wide(xx * 2 + hh, 512)]

    sends = []

    def go(src, dst, send, recv, target):
        copy = remote(src, dst, send, recv, target)
        copy.start()
        sends.append(copy)

    x1, x2, x3 = (x + 1) % 4, (x + 2) % 4, (x + 3) % 4
    go(og_ref, og_at(x, zh), o_send.at[0], o_recv.at[0], far)
    go(og_ref, og_at(x, zh), o_send.at[1], o_recv.at[1], right)
    go(og_ref, og_at(x, zh), o_send.at[2], o_recv.at[2], left)
    for d in range(3):
        go(w_ref, w_at(y, zl, c), w_send.at[d], w_recv.at[d], lines[d])
    go(w_ref, w_at(y, zl, c), w_send.at[3], w_recv.at[3], core)
    own_w = pltpu.make_async_copy(w_ref, w_at(y, zl, c), own_sem.at[0])
    own_w.start()
    own_og = pltpu.make_async_copy(og_ref, og_at(x, zh), own_sem.at[1])
    own_og.start()
    own_w.wait()
    number = 4
    for d in range(3):
        arrive(w_at(y, (zl + 3 - d) % 4, c), w_recv.at[d])
    for d in range(3):
        for k in range(4):
            zz = (zl + k) % 4
            go(w_at(y, zz, c), w_at(y, zz, c), w_send.at[number], w_recv.at[number], rings[d])
            number += 1
    for k in range(1, 4):
        zz = (zl + k) % 4
        go(w_at(y, zz, c), w_at(y, zz, c), w_send.at[number], w_recv.at[number], core)
        number += 1
    arrive(og_at(x3, zh), o_recv.at[1])
    go(og_half(x3, zh, 0), og_half(x3, zh, 0), o_send.at[3], o_recv.at[3], right)
    arrive(og_at(x1, zh), o_recv.at[2])
    go(og_half(x1, zh, 1), og_half(x1, zh, 1), o_send.at[4], o_recv.at[4], left)
    arrive(og_at(x, 1 - zh), o_recv.at[0])
    go(og_at(x, 1 - zh), og_at(x, 1 - zh), o_send.at[5], o_recv.at[5], right)
    go(og_at(x, 1 - zh), og_at(x, 1 - zh), o_send.at[6], o_recv.at[6], left)
    first = 4
    for d in range(3):
        for k in range(4):
            block = w_at((y + 3 - d) % 4, (zl + k) % 4, c)
            arrive(block, w_recv.at[first + 4 * d + k])
            go(block, block, w_send.at[number], w_recv.at[number], core)
            number += 1
    arrive(og_at(x3, 1 - zh), o_recv.at[5])
    go(og_half(x3, 1 - zh, 0), og_half(x3, 1 - zh, 0), o_send.at[7], o_recv.at[7], right)
    arrive(og_at(x1, 1 - zh), o_recv.at[6])
    go(og_half(x1, 1 - zh, 1), og_half(x1, 1 - zh, 1), o_send.at[8], o_recv.at[8], left)
    arrive(w_at(y, zl, 1 - c), w_recv.at[3])
    for k in range(1, 4):
        arrive(w_at(y, (zl + k) % 4, 1 - c), w_recv.at[15 + k])
    for d in range(3):
        for k in range(4):
            arrive(w_at((y + 3 - d) % 4, (zl + k) % 4, 1 - c), w_recv.at[19 + 4 * d + k])
    copy_w = pltpu.make_async_copy(w_buf, w_out, out_sem.at[0])
    copy_w.start()
    own_og.wait()
    arrive(og_half(x2, zh, 0), o_recv.at[3])
    arrive(og_half(x2, zh, 1), o_recv.at[4])
    arrive(og_half(x2, 1 - zh, 0), o_recv.at[7])
    arrive(og_half(x2, 1 - zh, 1), o_recv.at[8])
    copy_og = pltpu.make_async_copy(og_buf, og_out, out_sem.at[1])
    copy_og.start()

    @pl.loop(0, 3)
    def _(tile):
        rows = wide(tile, 256)
        gm_ref[rows, :] = lax.dot_general(
            og_buf[rows, :], w_buf[...], (((1,), (1,)), ((), ())), preferred_element_type=F32
        ).astype(BF16)

    for copy in sends:
        copy.wait_send()
    copy_w.wait()
    copy_og.wait()


def gather(weight_out, output_gradient):
    any_space = pl.BlockSpec(memory_space=pl.ANY)
    dma = pltpu.SemaphoreType.DMA
    return pl.pallas_call(
        gather_kernel,
        out_shape=(
            jax.ShapeDtypeStruct((512, 4096), BF16),
            jax.ShapeDtypeStruct((768, 4096), BF16),
            jax.ShapeDtypeStruct((768, 512), BF16),
        ),
        in_specs=[any_space, any_space],
        out_specs=(any_space, any_space, pl.BlockSpec(memory_space=pltpu.VMEM)),
        scratch_shapes=[
            pltpu.VMEM((512, 4096), BF16),
            pltpu.VMEM((768, 4096), BF16),
            dma((2,)),
            dma((31,)),
            dma((31,)),
            dma((9,)),
            dma((9,)),
            dma((2,)),
        ],
        compiler_params=pltpu.CompilerParams(
            collective_id=0, has_side_effects=True, vmem_limit_bytes=56 * 2**20
        ),
    )(weight_out, output_gradient)


def reduce_kernel(
    mixed_ref, w_ref, og_ref, out_ref, gw_ref,
    part, relay_l, relay_r, direct_l, direct_r, far_send, far_recv, total,
    gw_part, gw_core, gw_sum, gw_ring, gw_line, gw_last,
    x_send, x_recv, z_send, z_recv, g_send, g_recv,
):
    y, zl, c, x, zh = coords()
    core, lines, rings, right, left, far = neighbours()
    greet([core, *lines, *rings, right, left, far])
    x1, x2, x3 = (x + 1) % 4, (x + 2) % 4, (x + 3) % 4
    halves = (1 - zh, zh)
    top, low = pl.ds(0, 384), pl.ds(384, 384)
    sends = []

    def go(src, dst, send, recv, target):
        copy = remote(src, dst, send, recv, target)
        copy.start()
        sends.append(copy)

    def chunk(xx, k):
        return wide(xx * 2 + halves[k], 512)

    def project(xx, k):
        columns = chunk(xx, k)

        @pl.loop(0, 3)
        def _(tile):
            rows = wide(tile, 256)
            part[rows, columns] = jnp.dot(
                mixed_ref[rows, :], w_ref[:, columns], preferred_element_type=F32
            ).astype(BF16)

    for k in range(2):
        project(x2, k)
        go(part.at[top, chunk(x2, k)], relay_l.at[k], x_send.at[k], x_recv.at[k], right)
        go(part.at[low, chunk(x2, k)], relay_r.at[k], x_send.at[2 + k], x_recv.at[2 + k], left)
    for k in range(2):
        project(x1, k)
        go(part.at[low, chunk(x1, k)], direct_l.at[k, low], x_send.at[4 + k], x_recv.at[4 + k], right)
        project(x3, k)
        go(part.at[top, chunk(x3, k)], direct_r.at[k, top], x_send.at[6 + k], x_recv.at[6 + k], left)
    for k in range(2):
        project(x, k)

    def weights(group):
        @pl.loop(0, 2)
        def _(tile):
            rows = wide(tile, 256)
            value = lax.dot_general(
                mixed_ref[:, rows],
                og_ref[:, pl.ds(512 * group, 512)],
                (((0,), (0,)), ((), ())),
                preferred_element_type=F32,
            ).astype(BF16)
            for j in range(4):
                gw_part[j % 2, group // 2, (group % 2) * 2 + j // 2, rows, :] = value[:, 128 * j : 128 * j + 128]

    for group in range(8):
        weights(group)
    go(gw_part.at[1 - c], gw_core, g_send.at[0], g_recv.at[0], core)

    def relayed(k):
        arrive(relay_l.at[k], x_recv.at[k])
        part[top, chunk(x1, k)] = (part[top, chunk(x1, k)].astype(F32) + relay_l[k].astype(F32)).astype(BF16)
        go(part.at[top, chunk(x1, k)], direct_l.at[k, top], x_send.at[8 + k], x_recv.at[8 + k], right)
        arrive(relay_r.at[k], x_recv.at[2 + k])
        part[low, chunk(x3, k)] = (part[low, chunk(x3, k)].astype(F32) + relay_r[k].astype(F32)).astype(BF16)
        go(part.at[low, chunk(x3, k)], direct_r.at[k, low], x_send.at[10 + k], x_recv.at[10 + k], left)

    relayed(0)
    arrive(gw_core, g_recv.at[0])

    for d in (1, 2, 3, 0):
        yy = (y + d) % 4

        @pl.loop(0, 4)
        def _(z):
            gw_sum[yy, z] = (gw_part[c, yy, z].astype(F32) + gw_core[yy, z].astype(F32)).astype(BF16)

        if d:
            go(gw_sum.at[yy], gw_ring.at[d - 1], g_send.at[d], g_recv.at[d], rings[d - 1])

    relayed(1)

    def combined(k):
        arrive(direct_l.at[k, low], x_recv.at[4 + k])
        arrive(direct_r.at[k, top], x_recv.at[6 + k])
        arrive(direct_l.at[k, top], x_recv.at[8 + k])
        arrive(direct_r.at[k, low], x_recv.at[10 + k])
        return (
            part[:, chunk(x, k)].astype(F32) + direct_l[k].astype(F32) + direct_r[k].astype(F32)
        )

    far_send[...] = combined(0).astype(BF16)
    go(far_send, far_recv, z_send.at[0], z_recv.at[0], far)
    for d in range(3):
        arrive(gw_ring.at[d], g_recv.at[d + 1])

    @pl.loop(0, 4)
    def _(z):
        gw_line[z] = (
            gw_sum[y, z].astype(F32)
            + gw_ring[0, z].astype(F32)
            + gw_ring[1, z].astype(F32)
            + gw_ring[2, z].astype(F32)
        ).astype(BF16)

    for d in range(3):
        go(gw_line.at[(zl + d + 1) % 4], gw_last.at[d], g_send.at[4 + d], g_recv.at[4 + d], lines[d])
    total[...] = combined(1)
    for d in range(3):
        arrive(gw_last.at[d], g_recv.at[4 + d])
    gw_ref[...] = (
        gw_line[zl].astype(F32) + gw_last[0].astype(F32) + gw_last[1].astype(F32) + gw_last[2].astype(F32)
    ).astype(BF16)
    arrive(far_recv, z_recv.at[0])
    out_ref[...] = (total[...] + far_recv[...].astype(F32)).astype(BF16)
    for copy in sends:
        copy.wait_send()


def reduce(mixed, w_full, og_full):
    vmem = pl.BlockSpec(memory_space=pltpu.VMEM)
    dma = pltpu.SemaphoreType.DMA
    return pl.pallas_call(
        reduce_kernel,
        out_shape=(jax.ShapeDtypeStruct((768, 512), BF16), jax.ShapeDtypeStruct((512, 128), BF16)),
        in_specs=[vmem] * 3,
        out_specs=(vmem, vmem),
        scratch_shapes=[
            pltpu.VMEM((768, 4096), BF16),
            pltpu.VMEM((2, 384, 512), BF16),
            pltpu.VMEM((2, 384, 512), BF16),
            pltpu.VMEM((2, 768, 512), BF16),
            pltpu.VMEM((2, 768, 512), BF16),
            pltpu.VMEM((768, 512), BF16),
            pltpu.VMEM((768, 512), BF16),
            pltpu.VMEM((768, 512), F32),
            pltpu.VMEM((2, 4, 4, 512, 128), BF16),
            pltpu.VMEM((4, 4, 512, 128), BF16),
            pltpu.VMEM((4, 4, 512, 128), BF16),
            pltpu.VMEM((3, 4, 512, 128), BF16),
            pltpu.VMEM((4, 512, 128), BF16),
            pltpu.VMEM((3, 512, 128), BF16),
            dma((12,)),
            dma((12,)),
            dma((1,)),
            dma((1,)),
            dma((7,)),
            dma((7,)),
        ],
        compiler_params=pltpu.CompilerParams(
            collective_id=1, has_side_effects=True, vmem_limit_bytes=60 * 2**20
        ),
    )(mixed, w_full, og_full)


def shifted(value, axis, steps):
    count = lax.axis_size(axis)
    initial, last = (max(0, -steps), min(count, count - steps))
    return lax.ppermute(value, axis, [(source, source + steps) for source in range(initial, last)])


def attend(queries, keys, values, grad_out, permitted_mask, factor):
    scores = (
        jnp.einsum("bqhe,bkhe->bhqk", queries, keys, preferred_element_type=jnp.float32) * factor
    )
    scores = jnp.where(permitted_mask, scores, -1e30)
    highest = jnp.max(scores, axis=-1, keepdims=True)
    weights = jnp.exp(scores - highest)
    probs = (weights / jnp.sum(weights, axis=-1, keepdims=True)).astype(jnp.bfloat16)
    outputs = jnp.einsum(
        "bhqk,bkhe->bqhe", probs, values, preferred_element_type=jnp.float32
    ).astype(jnp.bfloat16)
    grad_probs = jnp.einsum("bqhe,bkhe->bhqk", grad_out, values, preferred_element_type=jnp.float32)
    centre = jnp.einsum("bqhe,bqhe->bhq", grad_out, outputs, preferred_element_type=jnp.float32)[
        ..., None
    ]
    grad_scores = (probs.astype(jnp.float32) * (grad_probs - centre)).astype(jnp.bfloat16)
    grad_queries = (
        jnp.einsum("bhqk,bkhe->bqhe", grad_scores, keys, preferred_element_type=jnp.float32)
        * factor
    )
    grad_keys = (
        jnp.einsum("bhqk,bqhe->bkhe", grad_scores, queries, preferred_element_type=jnp.float32)
        * factor
    )
    grad_values = jnp.einsum("bhqk,bqhe->bkhe", probs, grad_out, preferred_element_type=jnp.float32)
    return (outputs, grad_queries, grad_keys, grad_values)


def per_device(query, key, value, weight_out, output_gradient):
    token_stream = query.shape[0]
    features = query.shape[1]
    half_width = features // 2
    head_halves = half_width // HEAD_WIDTH
    local_rows = token_stream // ROW_LENGTH
    sequence_count = lax.axis_size("seq")
    all_rows = local_rows * sequence_count
    column_width = ROW_LENGTH // sequence_count
    factor = HEAD_WIDTH ** (-0.5)
    weight_rows, grad_full, grad_mixed = gather(weight_out, output_gradient)

    def rows_of(input_tensor):
        return input_tensor[:, :half_width].reshape(local_rows, ROW_LENGTH, head_halves, HEAD_WIDTH)

    def cols_of(input_tensor):
        return input_tensor[:, half_width:].reshape(local_rows, ROW_LENGTH, half_width)

    packed = jnp.stack([cols_of(query), cols_of(key), cols_of(value), cols_of(grad_mixed)])
    arrived = lax.all_to_all(packed, "seq", split_axis=2, concat_axis=1, tiled=True)
    row_query = rows_of(query)
    row_key = rows_of(key)
    row_value = rows_of(value)
    row_grad = rows_of(grad_mixed)
    token_position = jnp.arange(ROW_LENGTH)[:, None]
    target_index = jnp.arange(2 * ROW_LENGTH)[None, :]
    attention_window = (target_index > token_position) & (
        target_index <= token_position + ROW_LENGTH
    )
    border_rows = jnp.stack(
        [
            key[token_stream - ROW_LENGTH :, :half_width],
            value[token_stream - ROW_LENGTH :, :half_width],
        ]
    )
    prior_rows = shifted(border_rows, "seq", 1).reshape(2, ROW_LENGTH, head_halves, HEAD_WIDTH)
    row_keys = jnp.concatenate(
        [jnp.concatenate([prior_rows[0][None], row_key[:-1]], axis=0), row_key], axis=1
    )
    row_values = jnp.concatenate(
        [jnp.concatenate([prior_rows[1][None], row_value[:-1]], axis=0), row_value], axis=1
    )
    initial_window = (jnp.arange(local_rows) == 0) & (lax.axis_index("seq") == 0)
    permitted_mask = attention_window[None, None] & (
        (target_index >= ROW_LENGTH)[None, None]
        | jnp.logical_not(initial_window)[:, None, None, None]
    )
    row_out, row_gquery, row_key_gradient, row_value_gradient = attend(
        row_query, row_keys, row_values, row_grad, permitted_mask, factor
    )

    def settle_local(value_portion):
        subsequent_rows = jnp.concatenate(
            [value_portion[1:, :ROW_LENGTH], jnp.zeros_like(value_portion[:1, :ROW_LENGTH])], axis=0
        )
        return value_portion[:, ROW_LENGTH:] + subsequent_rows

    own_key = settle_local(row_key_gradient)
    own_value = settle_local(row_value_gradient)
    return_block = jnp.stack(
        [row_key_gradient[0, :ROW_LENGTH], row_value_gradient[0, :ROW_LENGTH]]
    ).reshape(2, ROW_LENGTH, half_width)
    incoming_block = (
        shifted(return_block.astype(jnp.bfloat16), "seq", -1)
        .astype(return_block.dtype)
        .reshape(2, ROW_LENGTH, head_halves, HEAD_WIDTH)
    )
    extra_key = incoming_block[0]
    extra_value = incoming_block[1]
    own_key = jnp.concatenate([own_key[:-1], own_key[-1:] + extra_key[None]], axis=0)
    own_value = jnp.concatenate([own_value[:-1], own_value[-1:] + extra_value[None]], axis=0)
    position_lattice = arrived.reshape(
        4, all_rows, column_width, head_halves, HEAD_WIDTH
    ).transpose(0, 2, 1, 3, 4)
    causal = jnp.arange(all_rows)[:, None] >= jnp.arange(all_rows)[None, :]
    col_out, col_gquery, col_gkey, col_gvalue = attend(
        position_lattice[0],
        position_lattice[1],
        position_lattice[2],
        position_lattice[3],
        causal[None, None],
        factor,
    )
    results = jnp.stack(
        [
            col_out,
            col_gquery.astype(jnp.bfloat16),
            col_gkey.astype(jnp.bfloat16),
            col_gvalue.astype(jnp.bfloat16),
        ]
    )
    results = results.transpose(0, 2, 1, 3, 4).reshape(4, all_rows, column_width, half_width)
    returned = lax.all_to_all(results, "seq", split_axis=1, concat_axis=2, tiled=True).reshape(
        4, token_stream, half_width
    )

    def join(row_portion, column_portion):
        return jnp.concatenate(
            [row_portion.reshape(token_stream, half_width), column_portion], axis=1
        )

    mixed = join(row_out, returned[0])
    grad_query = join(row_gquery.astype(jnp.bfloat16), returned[1])
    grad_key = join(own_key.astype(jnp.bfloat16), returned[2])
    grad_value = join(own_value.astype(jnp.bfloat16), returned[3])
    output, grad_weight = reduce(mixed, weight_rows, grad_full)
    return (output, grad_query, grad_key, grad_value, grad_weight)


def solution(mesh):
    in_specs = (P("seq", "mp"), P("seq", "mp"), P("seq", "mp"), P("mp", "seq"), P("seq", "mp"))
    out_specs = (P("seq", "mp"), P("seq", "mp"), P("seq", "mp"), P("seq", "mp"), P("mp", "seq"))
    return jax.shard_map(
        per_device, mesh=mesh, in_specs=in_specs, out_specs=out_specs, check_vma=False
    )
```

```python
import jax
import jax.numpy as jnp
from jax import lax
from jax.experimental import pallas as pl
from jax.experimental.pallas import tpu as pltpu
from jax.sharding import PartitionSpec as P

HEAD_WIDTH = 128
ROW_LENGTH = 256
MESH = pl.DeviceIdType.MESH
F32 = jnp.float32
BF16 = jnp.bfloat16


def coords():
    s = lax.axis_index("seq")
    m = lax.axis_index("mp")
    return s // 8, (s // 2) % 4, s % 2, m // 2, m % 2


def device(y, zl, c, x, zh):
    return (y * 8 + zl * 2 + c, x * 2 + zh)


def remote(src, dst, send, recv, target):
    return pltpu.make_async_remote_copy(
        src_ref=src, dst_ref=dst, send_sem=send, recv_sem=recv, device_id=target, device_id_type=MESH
    )


def arrive(ref, sem):
    pltpu.make_async_copy(ref, ref, sem).wait()


def wide(index, width):
    return pl.ds(pl.multiple_of(index * width, width), width)


def dot(a, b, left, right):
    return lax.dot_general(a, b, (((left,), (right,)), ((), ())), preferred_element_type=F32)


def layer_kernel(
    q_ref, k_ref, v_ref, w_ref, og_ref,
    out_ref, gq_ref, gk_ref, gv_ref, gw_ref,
    w_buf, og_buf, row_q, row_k, row_v, row_p, gm, mixed, gk_sum, gv_sum, edge_out, edge_in,
    col_in, col_gm, col_out, col_f, col_p,
    part, relay_l, relay_r, direct_l, direct_r, far_send, far_recv, total,
    gw_part, gw_core, gw_sum, gw_ring, gw_line, gw_last,
    own_sem, w_send, w_recv, o_send, o_recv, b_send, b_recv, c_send, c_recv,
    x_send, x_recv, z_send, z_recv, g_send, g_recv,
):
    y, zl, c, x, zh = coords()
    s, m = lax.axis_index("seq"), lax.axis_index("mp")
    factor = HEAD_WIDTH ** (-0.5)
    core = device(y, zl, 1 - c, x, zh)
    lines = [device(y, (zl + d) % 4, c, x, zh) for d in (1, 2, 3)]
    rings = [device((y + d) % 4, zl, c, x, zh) for d in (1, 2, 3)]
    x1, x2, x3 = (x + 1) % 4, (x + 2) % 4, (x + 3) % 4
    right = device(y, zl, c, x1, zh)
    left = device(y, zl, c, x3, zh)
    far = device(y, zl, c, x, 1 - zh)
    after, before = ((s + 1) % 32, m), ((s + 31) % 32, m)

    barrier = pltpu.get_barrier_semaphore()
    for target in (right, left, far):
        pl.semaphore_signal(barrier, inc=1, device_id=target, device_id_type=MESH)

    @pl.loop(1, 32)
    def _(i):
        pl.semaphore_signal(barrier, inc=1, device_id=((s + i) % 32, m), device_id_type=MESH)

    pl.semaphore_wait(barrier, 34)

    sends = []

    def go(src, dst, send, recv, target):
        copy = remote(src, dst, send, recv, target)
        copy.start()
        sends.append(copy)

    def w_at(yy, zz, cc):
        return w_buf.at[:, wide(yy * 8 + zz * 2 + cc, 128)]

    def og_half(xx, hh, half):
        return og_buf.at[pl.ds(384 * half, 384), wide(xx * 2 + hh, 512)]

    def og_own(half):
        return og_ref.at[pl.ds(384 * half, 384)]

    local = []

    def keep(src, dst, sem):
        copy = pltpu.make_async_copy(src, dst, sem)
        copy.start()
        local.append(copy)

    for d in range(3):
        go(w_ref, w_at(y, zl, c), w_send.at[d], w_recv.at[d], lines[d])
    go(w_ref, w_at(y, zl, c), w_send.at[3], w_recv.at[3], core)
    go(og_own(0), og_half(x, zh, 0), o_send.at[0], o_recv.at[0], far)
    go(og_own(0), og_half(x, zh, 0), o_send.at[2], o_recv.at[2], right)
    go(og_own(1), og_half(x, zh, 1), o_send.at[4], o_recv.at[4], left)
    go(og_own(1), og_half(x, zh, 1), o_send.at[1], o_recv.at[1], far)
    go(og_own(1), og_half(x, zh, 1), o_send.at[3], o_recv.at[3], right)
    go(og_own(0), og_half(x, zh, 0), o_send.at[5], o_recv.at[5], left)
    row_part = pl.ds(0, 256)
    keep(q_ref.at[:, :, row_part], row_q, own_sem.at[0])
    keep(k_ref.at[:, :, row_part], row_k.at[pl.ds(1, 3)], own_sem.at[1])
    keep(v_ref.at[:, :, row_part], row_v.at[pl.ds(1, 3)], own_sem.at[2])
    keep(w_ref, w_at(y, zl, c), own_sem.at[3])
    keep(og_ref, og_buf.at[:, wide(m, 512)], own_sem.at[4])
    go(k_ref.at[2, :, row_part], row_k.at[0], b_send.at[0], b_recv.at[0], after)
    go(v_ref.at[2, :, row_part], row_v.at[0], b_send.at[1], b_recv.at[1], after)

    def spot(ref, owner):
        return ref.at[:, wide(owner // 2, 16), pl.ds(pl.multiple_of(256 + 128 * (owner % 2), 128), 128)]

    def to_columns(pairs, number):
        @pl.loop(1, 32)
        def _(i):
            peer = (s + i) % 32
            for src, dst in pairs:
                remote(
                    spot(src, peer), dst.at[pl.ds(3 * s, 3)], c_send.at[number], c_recv.at[number], (peer, m)
                ).start()

        for src, dst in pairs:
            pltpu.make_async_copy(spot(src, s), dst.at[pl.ds(3 * s, 3)], c_recv.at[number]).start()

    def to_rows(pairs, number):
        @pl.loop(1, 32)
        def _(i):
            peer = (s + i) % 32
            for n, (src, dst) in enumerate(pairs):
                remote(
                    src.at[pl.ds(3 * peer, 3)], spot(dst, s), c_send.at[number + n], c_recv.at[number + n], (peer, m)
                ).start()

        for n, (src, dst) in enumerate(pairs):
            pltpu.make_async_copy(src.at[pl.ds(3 * s, 3)], spot(dst, s), c_recv.at[number + n]).start()

    to_columns([(q_ref, col_in.at[0]), (k_ref, col_in.at[1]), (v_ref, col_in.at[2])], 0)

    seen = lax.broadcasted_iota(jnp.int32, (256, 256), 0) >= lax.broadcasted_iota(jnp.int32, (256, 256), 1)

    def head(h):
        return pl.ds(pl.multiple_of(128 * h, 128), 128)

    def row_forward(t, h):
        queries = row_q[t, :, head(h)]
        own = dot(queries, row_k[t + 1, :, head(h)], 1, 1)
        prior = dot(queries, row_k[t, :, head(h)], 1, 1)
        open_side = jnp.logical_or(t > 0, s > 0)
        prior = jnp.where(open_side, prior * factor, -1e30)
        scores = jnp.where(seen, own * factor, prior)
        weights = jnp.exp(scores - jnp.max(scores, axis=-1, keepdims=True))
        probs = (weights / jnp.sum(weights, axis=-1, keepdims=True)).astype(BF16)
        row_p[t, h] = probs
        zero = jnp.zeros_like(probs)
        outputs = dot(jnp.where(seen, probs, zero), row_v[t + 1, :, head(h)], 1, 0) + dot(
            jnp.where(seen, zero, probs), row_v[t, :, head(h)], 1, 0
        )
        mixed[t, :, head(h)] = outputs.astype(BF16)

    def row_backward(t, h):
        queries, probs, grads = row_q[t, :, head(h)], row_p[t, h], gm[t, :, head(h)]
        own = dot(grads, row_v[t + 1, :, head(h)], 1, 1)
        prior = dot(grads, row_v[t, :, head(h)], 1, 1)
        centre = jnp.sum(grads.astype(F32) * mixed[t, :, head(h)].astype(F32), axis=-1, keepdims=True)
        slopes = (probs.astype(F32) * (jnp.where(seen, own, prior) - centre)).astype(BF16)
        zero = jnp.zeros_like(probs)
        slopes_own, slopes_prior = jnp.where(seen, slopes, zero), jnp.where(seen, zero, slopes)
        probs_own, probs_prior = jnp.where(seen, probs, zero), jnp.where(seen, zero, probs)
        gq_ref[t, :, head(h)] = (
            (dot(slopes_own, row_k[t + 1, :, head(h)], 1, 0) + dot(slopes_prior, row_k[t, :, head(h)], 1, 0))
            * factor
        ).astype(BF16)
        gk_sum[t, :, head(h)] += dot(slopes_prior, queries, 0, 0)
        gv_sum[t, :, head(h)] += dot(probs_prior, grads, 0, 0)
        gk_sum[t + 1, :, head(h)] = dot(slopes_own, queries, 0, 0)
        gv_sum[t + 1, :, head(h)] = dot(probs_own, grads, 0, 0)

    below = lax.broadcasted_iota(jnp.int32, (96, 96), 0) >= lax.broadcasted_iota(jnp.int32, (96, 96), 1)

    def widen(src, dst):
        @pl.loop(0, 6)
        def _(i):
            dst[wide(i, 256), :] = src[wide(i, 16)].astype(F32).reshape(256, 128)

    def narrow(src, dst):
        @pl.loop(0, 6)
        def _(i):
            dst[wide(i, 16)] = src[wide(i, 256), :].astype(BF16).reshape(16, 16, 128)

    def column(j):
        return pl.ds(j, 96, stride=16)

    def col_forward(j):
        queries, keys, values = (col_f[a, column(j), :].astype(BF16) for a in range(3))
        scores = jnp.where(below, dot(queries, keys, 1, 1) * factor, -1e30)
        weights = jnp.exp(scores - jnp.max(scores, axis=-1, keepdims=True))
        probs = (weights / jnp.sum(weights, axis=-1, keepdims=True)).astype(BF16)
        col_p[j] = probs
        col_f[3, column(j), :] = dot(probs, values, 1, 0).astype(BF16).astype(F32)

    def col_backward(j):
        queries, keys, values = (col_f[a, column(j), :].astype(BF16) for a in range(3))
        outputs, wide_grads = col_f[3, column(j), :], col_f[4, column(j), :]
        probs, grads = col_p[j], wide_grads.astype(BF16)
        centre = jnp.sum(wide_grads * outputs, axis=-1, keepdims=True)
        slopes = (probs.astype(F32) * (dot(grads, values, 1, 1) - centre)).astype(BF16)
        col_f[0, column(j), :] = dot(slopes, keys, 1, 0) * factor
        col_f[1, column(j), :] = dot(slopes, queries, 0, 0) * factor
        col_f[2, column(j), :] = dot(probs, grads, 0, 0)

    def columns_of(body):
        @pl.loop(0, 4)
        def _(g):
            for b in range(4):
                body(4 * g + b)

    def add_gm(xx, hh, first=False):
        @pl.loop(0, 3)
        def _(t):
            value = dot(og_buf[wide(t, 256), wide(xx * 2 + hh, 512)], w_buf[:, wide(xx * 2 + hh, 512)], 1, 1)
            if first:
                total[t] = value
            else:
                total[t] += value

    halves = (1 - zh, zh)
    top, low = pl.ds(0, 384), pl.ds(384, 384)

    def chunk(xx, k):
        return wide(xx * 2 + halves[k], 512)

    def project(xx, k):
        columns = chunk(xx, k)

        @pl.loop(0, 3)
        def _(t):
            part[wide(t, 256), columns] = jnp.dot(
                mixed[t], w_buf[:, columns], preferred_element_type=F32
            ).astype(BF16)

    for copy in local[:3]:
        copy.wait()

    @pl.loop(2, 6)
    def _(u):
        row_forward(u // 2, u % 2)

    arrive(og_half(x3, zh, 0), o_recv.at[2])
    go(og_half(x3, zh, 0), og_half(x3, zh, 0), o_send.at[6], o_recv.at[6], right)
    arrive(og_half(x1, zh, 1), o_recv.at[4])
    go(og_half(x1, zh, 1), og_half(x1, zh, 1), o_send.at[7], o_recv.at[7], left)
    local[3].wait()
    number = 4
    for d in range(3):
        arrive(w_at(y, (zl + 3 - d) % 4, c), w_recv.at[d])
    for d in range(3):
        for k in range(4):
            block = w_at(y, (zl + k) % 4, c)
            go(block, block, w_send.at[number], w_recv.at[number], rings[d])
            number += 1
    for k in range(1, 4):
        block = w_at(y, (zl + k) % 4, c)
        go(block, block, w_send.at[number], w_recv.at[number], core)
        number += 1
    for b in range(2):
        arrive((row_k, row_v)[b].at[0], b_recv.at[b])

    @pl.loop(0, 2)
    def _(h):
        row_forward(0, h)

    for half in range(2):
        block = og_half(x, 1 - zh, half)
        arrive(block, o_recv.at[half])
        go(block, block, o_send.at[8 + half], o_recv.at[8 + half], right)
        go(block, block, o_send.at[10 + half], o_recv.at[10 + half], left)
    arrive(col_in, c_recv.at[0])
    for a in range(3):
        widen(col_in.at[a], col_f.at[a])
    columns_of(col_forward)
    narrow(col_f.at[3], col_out.at[0])
    to_rows([(col_out.at[0], mixed)], 1)
    for d in range(3):
        for k in range(4):
            block = w_at((y + 3 - d) % 4, (zl + k) % 4, c)
            arrive(block, w_recv.at[4 + 4 * d + k])
            go(block, block, w_send.at[number], w_recv.at[number], core)
            number += 1
    arrive(og_half(x3, 1 - zh, 0), o_recv.at[8])
    go(og_half(x3, 1 - zh, 0), og_half(x3, 1 - zh, 0), o_send.at[12], o_recv.at[12], right)
    arrive(og_half(x1, 1 - zh, 1), o_recv.at[11])
    go(og_half(x1, 1 - zh, 1), og_half(x1, 1 - zh, 1), o_send.at[13], o_recv.at[13], left)
    arrive(w_at(y, zl, 1 - c), w_recv.at[3])
    for k in range(1, 4):
        arrive(w_at(y, (zl + k) % 4, 1 - c), w_recv.at[15 + k])
    for d in range(3):
        for k in range(4):
            arrive(w_at((y + 3 - d) % 4, (zl + k) % 4, 1 - c), w_recv.at[19 + 4 * d + k])
    local[4].wait()
    add_gm(x, zh, True)
    arrive(og_half(x3, zh, 1), o_recv.at[3])
    add_gm(x3, zh)
    arrive(og_half(x1, zh, 0), o_recv.at[5])
    add_gm(x1, zh)
    arrive(og_half(x2, zh, 0), o_recv.at[6])
    arrive(og_half(x2, zh, 1), o_recv.at[7])
    add_gm(x2, zh)
    add_gm(x, 1 - zh)

    arrive(mixed.at[:, :, pl.ds(256, 256)], c_recv.at[1])
    for k in range(2):
        project(x2, k)
        go(part.at[top, chunk(x2, k)], relay_l.at[k], x_send.at[k], x_recv.at[k], right)
        go(part.at[low, chunk(x2, k)], relay_r.at[k], x_send.at[2 + k], x_recv.at[2 + k], left)
    arrive(og_half(x3, 1 - zh, 1), o_recv.at[9])
    add_gm(x3, 1 - zh)
    arrive(og_half(x1, 1 - zh, 0), o_recv.at[10])
    add_gm(x1, 1 - zh)
    arrive(og_half(x2, 1 - zh, 0), o_recv.at[12])
    arrive(og_half(x2, 1 - zh, 1), o_recv.at[13])
    add_gm(x2, 1 - zh)

    @pl.loop(0, 3)
    def _(t):
        gm[t] = total[t].astype(BF16)

    to_columns([(gm, col_gm)], 2)
    for k in range(2):
        project(x1, k)
        go(part.at[low, chunk(x1, k)], direct_l.at[k, low], x_send.at[4 + k], x_recv.at[4 + k], right)
        project(x3, k)
        go(part.at[top, chunk(x3, k)], direct_r.at[k, top], x_send.at[6 + k], x_recv.at[6 + k], left)

    def relayed(k):
        arrive(relay_l.at[k], x_recv.at[k])
        part[top, chunk(x1, k)] = (part[top, chunk(x1, k)].astype(F32) + relay_l[k].astype(F32)).astype(BF16)
        go(part.at[top, chunk(x1, k)], direct_l.at[k, top], x_send.at[8 + k], x_recv.at[8 + k], right)
        arrive(relay_r.at[k], x_recv.at[2 + k])
        part[low, chunk(x3, k)] = (part[low, chunk(x3, k)].astype(F32) + relay_r[k].astype(F32)).astype(BF16)
        go(part.at[low, chunk(x3, k)], direct_r.at[k, low], x_send.at[10 + k], x_recv.at[10 + k], left)

    relayed(0)
    gk_sum[0] = jnp.zeros_like(gk_sum[0])
    gv_sum[0] = jnp.zeros_like(gv_sum[0])

    @pl.loop(0, 2)
    def _(h):
        row_backward(0, h)

    edge_out[0] = (gk_sum[0] * factor).astype(BF16)
    edge_out[1] = gv_sum[0].astype(BF16)
    go(edge_out, edge_in, b_send.at[2], b_recv.at[2], before)
    arrive(col_gm, c_recv.at[2])
    widen(col_gm, col_f.at[4])
    columns_of(col_backward)
    for a in range(3):
        narrow(col_f.at[a], col_out.at[a + 1])
    to_rows([(col_out.at[1], gq_ref), (col_out.at[2], gk_ref), (col_out.at[3], gv_ref)], 3)
    relayed(1)
    for k in range(2):
        project(x, k)

    for group in range(8):

        @pl.loop(0, 2)
        def _(tile):
            rows = wide(tile, 256)
            value = jnp.zeros((256, 512), F32)
            for t in range(3):
                value += dot(mixed[t, :, rows], og_buf[pl.ds(256 * t, 256), pl.ds(512 * group, 512)], 0, 0)
            value = value.astype(BF16)
            for j in range(4):
                gw_part[j % 2, group // 2, (group % 2) * 2 + j // 2, rows, :] = value[:, 128 * j : 128 * j + 128]

    go(gw_part.at[1 - c], gw_core, g_send.at[0], g_recv.at[0], core)

    def combined(k, t):
        rows = wide(t, 256)
        return (
            part[rows, chunk(x, k)].astype(F32) + direct_l[k, rows].astype(F32) + direct_r[k, rows].astype(F32)
        )

    def ready(k):
        arrive(direct_l.at[k, low], x_recv.at[4 + k])
        arrive(direct_r.at[k, top], x_recv.at[6 + k])
        arrive(direct_l.at[k, top], x_recv.at[8 + k])
        arrive(direct_r.at[k, low], x_recv.at[10 + k])

    ready(0)

    @pl.loop(0, 3)
    def _(t):
        far_send[t] = combined(0, t).astype(BF16)

    go(far_send, far_recv, z_send.at[0], z_recv.at[0], far)
    arrive(gw_core, g_recv.at[0])

    for d in (1, 2, 3, 0):
        yy = (y + d) % 4

        @pl.loop(0, 4)
        def _(z):
            gw_sum[yy, z] = (gw_part[c, yy, z].astype(F32) + gw_core[yy, z].astype(F32)).astype(BF16)

        if d:
            go(gw_sum.at[yy], gw_ring.at[d - 1], g_send.at[d], g_recv.at[d], rings[d - 1])

    @pl.loop(2, 6)
    def _(u):
        row_backward(u // 2, u % 2)

    ready(1)

    @pl.loop(0, 3)
    def _(t):
        total[t] = combined(1, t)

    for d in range(3):
        arrive(gw_ring.at[d], g_recv.at[d + 1])

    @pl.loop(0, 4)
    def _(z):
        gw_line[z] = (
            gw_sum[y, z].astype(F32)
            + gw_ring[0, z].astype(F32)
            + gw_ring[1, z].astype(F32)
            + gw_ring[2, z].astype(F32)
        ).astype(BF16)

    for d in range(3):
        go(gw_line.at[(zl + d + 1) % 4], gw_last.at[d], g_send.at[4 + d], g_recv.at[4 + d], lines[d])

    arrive(edge_in, b_recv.at[2])

    @pl.loop(0, 3)
    def _(t):
        edge_k = jnp.where(t == 2, edge_in[0].astype(F32), 0.0)
        edge_v = jnp.where(t == 2, edge_in[1].astype(F32), 0.0)
        gk_ref[t, :, row_part] = (gk_sum[t + 1] * factor + edge_k).astype(BF16)
        gv_ref[t, :, row_part] = (gv_sum[t + 1] + edge_v).astype(BF16)

    for d in range(3):
        arrive(gw_last.at[d], g_recv.at[4 + d])
    gw_ref[...] = (
        gw_line[zl].astype(F32) + gw_last[0].astype(F32) + gw_last[1].astype(F32) + gw_last[2].astype(F32)
    ).astype(BF16)
    arrive(far_recv, z_recv.at[0])

    @pl.loop(0, 3)
    def _(t):
        out_ref[t] = (total[t] + far_recv[t].astype(F32)).astype(BF16)

    for n, ref in enumerate((gq_ref, gk_ref, gv_ref)):
        arrive(ref.at[:, :, pl.ds(256, 256)], c_recv.at[3 + n])
    arrive(col_in.at[:, pl.ds(0, 93)], c_send.at[0])
    arrive(col_out.at[0, pl.ds(0, 93)], c_send.at[1])
    arrive(col_gm.at[pl.ds(0, 93)], c_send.at[2])
    for n in range(3):
        arrive(col_out.at[n + 1, pl.ds(0, 93)], c_send.at[3 + n])
    for copy in sends:
        copy.wait_send()


def per_device(query, key, value, weight_out, output_gradient):
    rows = jax.ShapeDtypeStruct((3, 256, 512), BF16)
    any_space = pl.BlockSpec(memory_space=pl.ANY)
    vmem = pl.BlockSpec(memory_space=pltpu.VMEM)
    dma = pltpu.SemaphoreType.DMA

    def half(*shape):
        return pltpu.VMEM(shape, BF16)

    def full(*shape):
        return pltpu.VMEM(shape, F32)

    output, grad_query, grad_key, grad_value, grad_weight = pl.pallas_call(
        layer_kernel,
        out_shape=(rows, rows, rows, rows, jax.ShapeDtypeStruct((512, 128), BF16)),
        in_specs=[any_space] * 5,
        out_specs=(vmem,) * 5,
        scratch_shapes=[
            half(512, 4096),
            half(768, 4096),
            half(3, 256, 256),
            half(4, 256, 256),
            half(4, 256, 256),
            half(3, 2, 256, 256),
            half(3, 256, 512),
            half(3, 256, 512),
            full(4, 256, 256),
            full(4, 256, 256),
            half(2, 256, 256),
            half(2, 256, 256),
            half(3, 96, 16, 128),
            half(96, 16, 128),
            half(4, 96, 16, 128),
            full(5, 1536, 128),
            half(16, 96, 96),
            half(768, 4096),
            half(2, 384, 512),
            half(2, 384, 512),
            half(2, 768, 512),
            half(2, 768, 512),
            half(3, 256, 512),
            half(3, 256, 512),
            full(3, 256, 512),
            half(2, 4, 4, 512, 128),
            half(4, 4, 512, 128),
            half(4, 4, 512, 128),
            half(3, 4, 512, 128),
            half(4, 512, 128),
            half(3, 512, 128),
            dma((5,)),
            dma((31,)),
            dma((31,)),
            dma((14,)),
            dma((14,)),
            dma((3,)),
            dma((3,)),
            dma((6,)),
            dma((6,)),
            dma((12,)),
            dma((12,)),
            dma((1,)),
            dma((1,)),
            dma((7,)),
            dma((7,)),
        ],
        compiler_params=pltpu.CompilerParams(
            collective_id=0, has_side_effects=True, vmem_limit_bytes=62 * 2**20
        ),
    )(
        query.reshape(3, 256, 512),
        key.reshape(3, 256, 512),
        value.reshape(3, 256, 512),
        weight_out,
        output_gradient,
    )
    return (
        output.reshape(768, 512),
        grad_query.reshape(768, 512),
        grad_key.reshape(768, 512),
        grad_value.reshape(768, 512),
        grad_weight,
    )


def solution(mesh):
    in_specs = (P("seq", "mp"), P("seq", "mp"), P("seq", "mp"), P("mp", "seq"), P("seq", "mp"))
    out_specs = (P("seq", "mp"), P("seq", "mp"), P("seq", "mp"), P("seq", "mp"), P("mp", "seq"))
    return jax.shard_map(
        per_device, mesh=mesh, in_specs=in_specs, out_specs=out_specs, check_vma=False
    )
```

```python
import jax
import jax.numpy as jnp
from jax import lax
from jax.experimental import pallas as pl
from jax.experimental.pallas import tpu as pltpu
from jax.sharding import PartitionSpec as P

HEAD_WIDTH = 128
ROW_LENGTH = 256
MESH = pl.DeviceIdType.MESH
F32 = jnp.float32
BF16 = jnp.bfloat16


def coords():
    s = lax.axis_index("seq")
    m = lax.axis_index("mp")
    return s // 8, (s // 2) % 4, s % 2, m // 2, m % 2


def device(y, zl, c, x, zh):
    return (y * 8 + zl * 2 + c, x * 2 + zh)


def remote(src, dst, send, recv, target):
    return pltpu.make_async_remote_copy(
        src_ref=src, dst_ref=dst, send_sem=send, recv_sem=recv, device_id=target, device_id_type=MESH
    )


def arrive(ref, sem):
    pltpu.make_async_copy(ref, ref, sem).wait()


def wide(index, width):
    return pl.ds(pl.multiple_of(index * width, width), width)


def dot(a, b, left, right):
    return lax.dot_general(a, b, (((left,), (right,)), ((), ())), preferred_element_type=F32)


def layer_kernel(
    q_ref, k_ref, v_ref, w_ref, og_ref,
    out_ref, gq_ref, gk_ref, gv_ref, gw_ref,
    w_buf, og_buf, row_q, row_k, row_v, row_p, gm_own, gm_far, gm_row, gm_in, mixed, mixed_far,
    gk_sum, gv_sum, edge_out, edge_in,
    col_in, col_gm, col_out, col_f, col_p,
    part, relay_l, relay_r, direct_l, direct_r, total,
    gw_part, gw_core, gw_sum, gw_ring, gw_line, gw_last,
    own_sem, w_send, w_recv, o_send, o_recv, b_send, b_recv, c_send, c_recv,
    x_send, x_recv, z_send, z_recv, g_send, g_recv,
):
    y, zl, c, x, zh = coords()
    s, m = lax.axis_index("seq"), lax.axis_index("mp")
    m_far = x * 2 + 1 - zh
    factor = HEAD_WIDTH ** (-0.5)
    core = device(y, zl, 1 - c, x, zh)
    rings = [device((y + d) % 4, zl, c, x, zh) for d in (1, 2, 3)]
    x1, x2, x3 = (x + 1) % 4, (x + 2) % 4, (x + 3) % 4
    right = device(y, zl, c, x1, zh)
    left = device(y, zl, c, x3, zh)
    far = device(y, zl, c, x, 1 - zh)
    after, before = ((s + 1) % 32, m), ((s + 31) % 32, m)
    user = zl // 2
    at_home = user == zh
    away = jnp.logical_not(at_home)

    barrier = pltpu.get_barrier_semaphore()
    for target in (right, left, far):
        pl.semaphore_signal(barrier, inc=1, device_id=target, device_id_type=MESH)

    @pl.loop(1, 32)
    def _(i):
        peer = (s + i) % 32
        pl.semaphore_signal(barrier, inc=1, device_id=(peer, m), device_id_type=MESH)
        pl.semaphore_signal(barrier, inc=1, device_id=(peer, m_far), device_id_type=MESH)

    pl.semaphore_wait(barrier, 65)

    sends = []

    def go(src, dst, send, recv, target):
        copy = remote(src, dst, send, recv, target)
        copy.start()
        sends.append(copy)

    def slot(yy, b, cc):
        return wide(yy * 4 + b * 2 + cc, 128)

    def og_half(xx, half):
        return og_buf.at[pl.ds(384 * half, 384), wide(xx, 512)]

    def og_own(half):
        return og_ref.at[pl.ds(384 * half, 384)]

    local = []

    def keep(src, dst, sem):
        copy = pltpu.make_async_copy(src, dst, sem)
        copy.start()
        local.append(copy)

    side = jnp.where(at_home, 0, 1)
    w_here = w_buf.at[side, :, slot(y, zl % 2, c)]
    w_index = side * 2 + zl % 2
    for d in range(1, 4):
        go(w_ref, w_here, w_send.at[d], w_recv.at[w_index], device(y, (zl + d) % 4, c, x, user))
    w_away = remote(w_ref, w_here, w_send.at[0], w_recv.at[w_index], far)
    w_home = pltpu.make_async_copy(w_ref, w_here, w_recv.at[w_index])

    @pl.when(away)
    def _():
        w_away.start()

    @pl.when(at_home)
    def _():
        w_home.start()

    go(og_own(0), og_half(x, 0), o_send.at[0], o_recv.at[0], right)
    go(og_own(1), og_half(x, 1), o_send.at[1], o_recv.at[1], left)
    go(og_own(1), og_half(x, 1), o_send.at[2], o_recv.at[2], right)
    go(og_own(0), og_half(x, 0), o_send.at[3], o_recv.at[3], left)
    row_part, col_part = pl.ds(0, 256), pl.ds(256, 256)
    keep(q_ref.at[:, :, row_part], row_q, own_sem.at[0])
    keep(k_ref.at[:, :, row_part], row_k.at[pl.ds(1, 3)], own_sem.at[1])
    keep(v_ref.at[:, :, row_part], row_v.at[pl.ds(1, 3)], own_sem.at[2])
    keep(og_ref, og_buf.at[:, wide(x, 512)], own_sem.at[3])
    go(k_ref.at[2, :, row_part], row_k.at[0], b_send.at[0], b_recv.at[0], after)
    go(v_ref.at[2, :, row_part], row_v.at[0], b_send.at[1], b_recv.at[1], after)

    def spot(ref, owner):
        return ref.at[:, wide(owner // 2, 16), pl.ds(pl.multiple_of(256 + 128 * (owner % 2), 128), 128)]

    def to_columns(pairs, number):
        @pl.loop(1, 32)
        def _(i):
            peer = (s + i) % 32
            for src, dst in pairs:
                remote(
                    spot(src, peer), dst.at[pl.ds(3 * s, 3)], c_send.at[number], c_recv.at[number], (peer, m)
                ).start()

        for src, dst in pairs:
            pltpu.make_async_copy(spot(src, s), dst.at[pl.ds(3 * s, 3)], c_recv.at[number]).start()

    def to_far_columns(src, dst, number):
        @pl.loop(0, 32)
        def _(i):
            peer = (s + i) % 32
            remote(
                spot(src, peer), dst.at[pl.ds(3 * s, 3)], c_send.at[number], c_recv.at[number], (peer, m_far)
            ).start()

    def to_rows(pairs, number):
        @pl.loop(1, 32)
        def _(i):
            peer = (s + i) % 32
            for n, (src, dst) in enumerate(pairs):
                remote(
                    src.at[pl.ds(3 * peer, 3)], spot(dst, s), c_send.at[number + n], c_recv.at[number + n], (peer, m)
                ).start()

        for n, (src, dst) in enumerate(pairs):
            pltpu.make_async_copy(src.at[pl.ds(3 * s, 3)], spot(dst, s), c_recv.at[number + n]).start()

    def to_far_rows(src, dst, number):
        @pl.loop(0, 32)
        def _(i):
            peer = (s + i) % 32
            remote(
                src.at[pl.ds(3 * peer, 3)], spot(dst, s), c_send.at[number], c_recv.at[number], (peer, m_far)
            ).start()

    to_columns([(q_ref, col_in.at[0]), (k_ref, col_in.at[1]), (v_ref, col_in.at[2])], 0)

    seen = lax.broadcasted_iota(jnp.int32, (256, 256), 0) >= lax.broadcasted_iota(jnp.int32, (256, 256), 1)

    def head(h):
        return pl.ds(pl.multiple_of(128 * h, 128), 128)

    def row_forward(t, h):
        queries = row_q[t, :, head(h)]
        own = dot(queries, row_k[t + 1, :, head(h)], 1, 1)
        prior = dot(queries, row_k[t, :, head(h)], 1, 1)
        open_side = jnp.logical_or(t > 0, s > 0)
        prior = jnp.where(open_side, prior * factor, -1e30)
        scores = jnp.where(seen, own * factor, prior)
        weights = jnp.exp(scores - jnp.max(scores, axis=-1, keepdims=True))
        probs = (weights / jnp.sum(weights, axis=-1, keepdims=True)).astype(BF16)
        row_p[t, h] = probs
        zero = jnp.zeros_like(probs)
        outputs = dot(jnp.where(seen, probs, zero), row_v[t + 1, :, head(h)], 1, 0) + dot(
            jnp.where(seen, zero, probs), row_v[t, :, head(h)], 1, 0
        )
        mixed[t, :, head(h)] = outputs.astype(BF16)

    def row_backward(t, h):
        queries, probs, grads = row_q[t, :, head(h)], row_p[t, h], gm_row[t, :, head(h)]
        own = dot(grads, row_v[t + 1, :, head(h)], 1, 1)
        prior = dot(grads, row_v[t, :, head(h)], 1, 1)
        centre = jnp.sum(grads.astype(F32) * mixed[t, :, head(h)].astype(F32), axis=-1, keepdims=True)
        slopes = (probs.astype(F32) * (jnp.where(seen, own, prior) - centre)).astype(BF16)
        zero = jnp.zeros_like(probs)
        slopes_own, slopes_prior = jnp.where(seen, slopes, zero), jnp.where(seen, zero, slopes)
        probs_own, probs_prior = jnp.where(seen, probs, zero), jnp.where(seen, zero, probs)
        gq_ref[t, :, head(h)] = (
            (dot(slopes_own, row_k[t + 1, :, head(h)], 1, 0) + dot(slopes_prior, row_k[t, :, head(h)], 1, 0))
            * factor
        ).astype(BF16)
        gk_sum[t, :, head(h)] += dot(slopes_prior, queries, 0, 0)
        gv_sum[t, :, head(h)] += dot(probs_prior, grads, 0, 0)
        gk_sum[t + 1, :, head(h)] = dot(slopes_own, queries, 0, 0)
        gv_sum[t + 1, :, head(h)] = dot(probs_own, grads, 0, 0)

    below = lax.broadcasted_iota(jnp.int32, (96, 96), 0) >= lax.broadcasted_iota(jnp.int32, (96, 96), 1)

    def widen(src, dst):
        @pl.loop(0, 6)
        def _(i):
            dst[wide(i, 256), :] = src[wide(i, 16)].astype(F32).reshape(256, 128)

    def narrow(src, dst):
        @pl.loop(0, 6)
        def _(i):
            dst[wide(i, 16)] = src[wide(i, 256), :].astype(BF16).reshape(16, 16, 128)

    def column(j):
        return pl.ds(j, 96, stride=16)

    def col_forward(j):
        queries, keys, values = (col_f[a, column(j), :].astype(BF16) for a in range(3))
        scores = jnp.where(below, dot(queries, keys, 1, 1) * factor, -1e30)
        weights = jnp.exp(scores - jnp.max(scores, axis=-1, keepdims=True))
        probs = (weights / jnp.sum(weights, axis=-1, keepdims=True)).astype(BF16)
        col_p[j] = probs
        col_f[3, column(j), :] = dot(probs, values, 1, 0).astype(BF16).astype(F32)

    def col_backward(j):
        queries, keys, values = (col_f[a, column(j), :].astype(BF16) for a in range(3))
        outputs, wide_grads = col_f[3, column(j), :], col_f[4, column(j), :]
        probs, grads = col_p[j], wide_grads.astype(BF16)
        centre = jnp.sum(wide_grads * outputs, axis=-1, keepdims=True)
        slopes = (probs.astype(F32) * (dot(grads, values, 1, 1) - centre)).astype(BF16)
        col_f[0, column(j), :] = dot(slopes, keys, 1, 0) * factor
        col_f[1, column(j), :] = dot(slopes, queries, 0, 0) * factor
        col_f[2, column(j), :] = dot(probs, grads, 0, 0)

    def columns_of(body):
        @pl.loop(0, 4)
        def _(g):
            for b in range(4):
                body(4 * g + b)

    top, low = pl.ds(0, 384), pl.ds(384, 384)

    def project(xx):
        columns = wide(xx, 512)

        @pl.loop(0, 3)
        def _(t):
            part[wide(t, 256), columns] = (
                dot(mixed[t], w_buf[0, :, columns], 1, 0) + dot(mixed_far[t], w_buf[1, :, columns], 1, 0)
            ).astype(BF16)

    for copy in local[:3]:
        copy.wait()

    @pl.loop(2, 6)
    def _(u):
        row_forward(u // 2, u % 2)

    arrive(og_half(x3, 0), o_recv.at[0])
    go(og_half(x3, 0), og_half(x3, 0), o_send.at[4], o_recv.at[4], right)
    arrive(og_half(x1, 1), o_recv.at[1])
    go(og_half(x1, 1), og_half(x1, 1), o_send.at[5], o_recv.at[5], left)
    for a in range(2):
        for b in range(2):
            arrive(w_buf.at[a, :, slot(y, b, c)], w_recv.at[2 * a + b])
    for d in range(3):
        for b in range(2):
            block = w_buf.at[:, :, slot(y, b, c)]
            go(block, block, w_send.at[4 + 2 * d + b], w_recv.at[4 + 2 * d + b], rings[d])
    for b in range(2):
        block = w_buf.at[:, :, slot(y, b, c)]
        go(block, block, w_send.at[10 + b], w_recv.at[10 + b], core)
    for b in range(2):
        arrive((row_k, row_v)[b].at[0], b_recv.at[b])

    @pl.loop(0, 2)
    def _(h):
        row_forward(0, h)

    arrive(col_in, c_recv.at[0])
    go(mixed.at[:, :, row_part], mixed_far.at[:, :, row_part], z_send.at[0], z_recv.at[0], far)
    for a in range(3):
        widen(col_in.at[a], col_f.at[a])
    columns_of(col_forward)
    narrow(col_f.at[3], col_out.at[0])
    to_rows([(col_out.at[0], mixed)], 1)
    to_far_rows(col_out.at[0], mixed_far, 6)
    for d in range(3):
        for b in range(2):
            block = w_buf.at[:, :, slot((y + 3 - d) % 4, b, c)]
            arrive(block, w_recv.at[4 + 2 * d + b])
            go(block, block, w_send.at[12 + 2 * d + b], w_recv.at[12 + 2 * d + b], core)
    local[3].wait()
    arrive(og_half(x3, 1), o_recv.at[2])
    arrive(og_half(x1, 0), o_recv.at[3])
    arrive(og_half(x2, 0), o_recv.at[4])
    arrive(og_half(x2, 1), o_recv.at[5])
    for b in range(2):
        arrive(w_buf.at[:, :, slot(y, b, 1 - c)], w_recv.at[10 + b])
    for d in range(3):
        for b in range(2):
            arrive(w_buf.at[:, :, slot((y + 3 - d) % 4, b, 1 - c)], w_recv.at[12 + 2 * d + b])

    @pl.loop(0, 3)
    def _(t):
        gm_far[t] = dot(og_buf[wide(t, 256), :], w_buf[1], 1, 1).astype(BF16)

    to_far_columns(gm_far, col_gm.at[1], 7)

    @pl.loop(0, 3)
    def _(t):
        value = dot(og_buf[wide(t, 256), :], w_buf[0], 1, 1)
        total[t] = value
        gm_own[t] = value.astype(BF16)

    to_columns([(gm_own, col_gm.at[0])], 2)
    go(gm_far.at[:, :, row_part], gm_in, z_send.at[1], z_recv.at[1], far)

    arrive(mixed_far.at[:, :, row_part], z_recv.at[0])
    arrive(mixed.at[:, :, col_part], c_recv.at[1])
    arrive(mixed_far.at[:, :, col_part], c_recv.at[6])
    project(x2)
    go(part.at[top, wide(x2, 512)], relay_l, x_send.at[0], x_recv.at[0], right)
    go(part.at[low, wide(x2, 512)], relay_r, x_send.at[1], x_recv.at[1], left)
    project(x1)
    go(part.at[low, wide(x1, 512)], direct_l.at[low], x_send.at[2], x_recv.at[2], right)
    project(x3)
    go(part.at[top, wide(x3, 512)], direct_r.at[top], x_send.at[3], x_recv.at[3], left)

    for a, ref in enumerate((mixed, mixed_far)):
        for group in range(4):

            @pl.loop(0, 2)
            def _(tile):
                rows = wide(tile, 256)
                value = jnp.zeros((256, 512), F32)
                for t in range(3):
                    value += dot(ref[t, :, rows], og_buf[pl.ds(256 * t, 256), pl.ds(512 * group, 512)], 0, 0)
                value = value.astype(BF16)
                for j in range(4):
                    gw_part[j % 2, group, j // 2, a, rows, :] = value[:, 128 * j : 128 * j + 128]

    go(gw_part.at[1 - c], gw_core, g_send.at[0], g_recv.at[0], core)
    arrive(relay_l, x_recv.at[0])
    part[top, wide(x1, 512)] = (part[top, wide(x1, 512)].astype(F32) + relay_l[...].astype(F32)).astype(BF16)
    go(part.at[top, wide(x1, 512)], direct_l.at[top], x_send.at[4], x_recv.at[4], right)
    arrive(relay_r, x_recv.at[1])
    part[low, wide(x3, 512)] = (part[low, wide(x3, 512)].astype(F32) + relay_r[...].astype(F32)).astype(BF16)
    go(part.at[low, wide(x3, 512)], direct_r.at[low], x_send.at[5], x_recv.at[5], left)

    arrive(col_gm.at[0], c_recv.at[2])
    arrive(col_gm.at[1], c_recv.at[7])

    @pl.loop(0, 6)
    def _(i):
        rows = wide(i, 16)
        value = (col_gm[0, rows].astype(F32) + col_gm[1, rows].astype(F32)).astype(BF16)
        col_f[4, wide(i, 256), :] = value.astype(F32).reshape(256, 128)

    columns_of(col_backward)
    for a in range(3):
        narrow(col_f.at[a], col_out.at[a + 1])
    to_rows([(col_out.at[1], gq_ref), (col_out.at[2], gk_ref), (col_out.at[3], gv_ref)], 3)

    arrive(gw_core, g_recv.at[0])
    for d in (1, 2, 3, 0):
        yy = (y + d) % 4

        @pl.loop(0, 2)
        def _(b):
            gw_sum[yy, b] = (gw_part[c, yy, b].astype(F32) + gw_core[yy, b].astype(F32)).astype(BF16)

        if d:
            go(gw_sum.at[yy], gw_ring.at[d - 1], g_send.at[d], g_recv.at[d], rings[d - 1])

    arrive(gm_in, z_recv.at[1])

    @pl.loop(0, 3)
    def _(t):
        gm_row[t] = (total[t, :, row_part] + gm_in[t].astype(F32)).astype(BF16)

    gk_sum[0] = jnp.zeros_like(gk_sum[0])
    gv_sum[0] = jnp.zeros_like(gv_sum[0])

    @pl.loop(0, 2)
    def _(h):
        row_backward(0, h)

    edge_out[0] = (gk_sum[0] * factor).astype(BF16)
    edge_out[1] = gv_sum[0].astype(BF16)
    go(edge_out, edge_in, b_send.at[2], b_recv.at[2], before)

    @pl.loop(2, 6)
    def _(u):
        row_backward(u // 2, u % 2)

    for d in range(3):
        arrive(gw_ring.at[d], g_recv.at[d + 1])

    @pl.loop(0, 2)
    def _(b):
        gw_line[b] = (
            gw_sum[y, b].astype(F32)
            + gw_ring[0, b].astype(F32)
            + gw_ring[1, b].astype(F32)
            + gw_ring[2, b].astype(F32)
        ).astype(BF16)

    ends = []
    for a in range(2):
        for b in range(2):
            owner = device(y, 2 * zh + b, c, x, zh if a == 0 else 1 - zh)
            copy = remote(
                gw_line.at[b, a], gw_last.at[zl], g_send.at[4 + 2 * a + b], g_recv.at[4 + zl], owner
            )
            if a == 0:
                other = zl != 2 * zh + b
                home = pltpu.make_async_copy(gw_line.at[b, a], gw_last.at[zl], g_recv.at[4 + zl])

                @pl.when(other)
                def _():
                    copy.start()

                @pl.when(jnp.logical_not(other))
                def _():
                    home.start()

                ends.append((other, copy))
            else:
                copy.start()
                sends.append(copy)

    project(x)
    arrive(direct_l.at[low], x_recv.at[2])
    arrive(direct_r.at[top], x_recv.at[3])
    arrive(direct_l.at[top], x_recv.at[4])
    arrive(direct_r.at[low], x_recv.at[5])

    @pl.loop(0, 3)
    def _(t):
        rows = wide(t, 256)
        out_ref[t] = (
            part[rows, wide(x, 512)].astype(F32) + direct_l[rows].astype(F32) + direct_r[rows].astype(F32)
        ).astype(BF16)

    arrive(edge_in, b_recv.at[2])

    @pl.loop(0, 3)
    def _(t):
        edge_k = jnp.where(t == 2, edge_in[0].astype(F32), 0.0)
        edge_v = jnp.where(t == 2, edge_in[1].astype(F32), 0.0)
        gk_ref[t, :, row_part] = (gk_sum[t + 1] * factor + edge_k).astype(BF16)
        gv_ref[t, :, row_part] = (gv_sum[t + 1] + edge_v).astype(BF16)

    for n, ref in enumerate((gq_ref, gk_ref, gv_ref)):
        arrive(ref.at[:, :, col_part], c_recv.at[3 + n])
    for z in range(4):
        arrive(gw_last.at[z], g_recv.at[4 + z])
    gw_ref[...] = (
        gw_last[0].astype(F32) + gw_last[1].astype(F32) + gw_last[2].astype(F32) + gw_last[3].astype(F32)
    ).astype(BF16)
    arrive(col_in.at[:, pl.ds(0, 93)], c_send.at[0])
    arrive(col_out.at[0, pl.ds(0, 93)], c_send.at[1])
    arrive(col_gm.at[0, pl.ds(0, 93)], c_send.at[2])
    for n in range(3):
        arrive(col_out.at[n + 1, pl.ds(0, 93)], c_send.at[3 + n])
    arrive(col_out.at[0], c_send.at[6])
    arrive(col_gm.at[0], c_send.at[7])
    for copy in sends:
        copy.wait_send()
    for other, copy in ends:

        @pl.when(other)
        def _():
            copy.wait_send()

    @pl.when(away)
    def _():
        w_away.wait_send()


def per_device(query, key, value, weight_out, output_gradient):
    rows = jax.ShapeDtypeStruct((3, 256, 512), BF16)
    any_space = pl.BlockSpec(memory_space=pl.ANY)
    vmem = pl.BlockSpec(memory_space=pltpu.VMEM)
    dma = pltpu.SemaphoreType.DMA

    def half(*shape):
        return pltpu.VMEM(shape, BF16)

    def full(*shape):
        return pltpu.VMEM(shape, F32)

    output, grad_query, grad_key, grad_value, grad_weight = pl.pallas_call(
        layer_kernel,
        out_shape=(rows, rows, rows, rows, jax.ShapeDtypeStruct((512, 128), BF16)),
        in_specs=[any_space] * 5,
        out_specs=(vmem,) * 5,
        scratch_shapes=[
            half(2, 512, 2048),
            half(768, 2048),
            half(3, 256, 256),
            half(4, 256, 256),
            half(4, 256, 256),
            half(3, 2, 256, 256),
            half(3, 256, 512),
            half(3, 256, 512),
            half(3, 256, 256),
            half(3, 256, 256),
            half(3, 256, 512),
            half(3, 256, 512),
            full(4, 256, 256),
            full(4, 256, 256),
            half(2, 256, 256),
            half(2, 256, 256),
            half(3, 96, 16, 128),
            half(2, 96, 16, 128),
            half(4, 96, 16, 128),
            full(5, 1536, 128),
            half(16, 96, 96),
            half(768, 2048),
            half(384, 512),
            half(384, 512),
            half(768, 512),
            half(768, 512),
            full(3, 256, 512),
            half(2, 4, 2, 2, 512, 128),
            half(4, 2, 2, 512, 128),
            half(4, 2, 2, 512, 128),
            half(3, 2, 2, 512, 128),
            half(2, 2, 512, 128),
            half(4, 512, 128),
            dma((4,)),
            dma((18,)),
            dma((18,)),
            dma((6,)),
            dma((6,)),
            dma((3,)),
            dma((3,)),
            dma((8,)),
            dma((8,)),
            dma((6,)),
            dma((6,)),
            dma((2,)),
            dma((2,)),
            dma((8,)),
            dma((8,)),
        ],
        compiler_params=pltpu.CompilerParams(
            collective_id=0, has_side_effects=True, vmem_limit_bytes=62 * 2**20
        ),
    )(
        query.reshape(3, 256, 512),
        key.reshape(3, 256, 512),
        value.reshape(3, 256, 512),
        weight_out,
        output_gradient,
    )
    return (
        output.reshape(768, 512),
        grad_query.reshape(768, 512),
        grad_key.reshape(768, 512),
        grad_value.reshape(768, 512),
        grad_weight,
    )


def solution(mesh):
    in_specs = (P("seq", "mp"), P("seq", "mp"), P("seq", "mp"), P("mp", "seq"), P("seq", "mp"))
    out_specs = (P("seq", "mp"), P("seq", "mp"), P("seq", "mp"), P("seq", "mp"), P("mp", "seq"))
    return jax.shard_map(
        per_device, mesh=mesh, in_specs=in_specs, out_specs=out_specs, check_vma=False
    )
```

```python
import jax
import jax.numpy as jnp
from jax import lax
from jax.experimental import pallas as pl
from jax.experimental.pallas import tpu as pltpu
from jax.sharding import PartitionSpec as P

HEAD_WIDTH = 128
ROW_LENGTH = 256
MESH = pl.DeviceIdType.MESH
F32 = jnp.float32
BF16 = jnp.bfloat16


def coords():
    s = lax.axis_index("seq")
    m = lax.axis_index("mp")
    return s // 8, (s // 2) % 4, s % 2, m // 2, m % 2


def device(y, zl, c, x, zh):
    return (y * 8 + zl * 2 + c, x * 2 + zh)


def remote(src, dst, send, recv, target):
    return pltpu.make_async_remote_copy(
        src_ref=src, dst_ref=dst, send_sem=send, recv_sem=recv, device_id=target, device_id_type=MESH
    )


def arrive(ref, sem):
    pltpu.make_async_copy(ref, ref, sem).wait()


def wide(index, width):
    return pl.ds(pl.multiple_of(index * width, width), width)


def dot(a, b, left, right):
    return lax.dot_general(a, b, (((left,), (right,)), ((), ())), preferred_element_type=F32)


def layer_kernel(
    q_ref, k_ref, v_ref, w_ref, og_ref,
    out_ref, gq_ref, gk_ref, gv_ref, gw_ref,
    w_buf, og_buf, row_q, row_k, row_v, row_p, gm_own, gm_far, gm_row, gm_in, mixed, mixed_far,
    gk_sum, gv_sum, edge_out, edge_in,
    col_in, col_gm, col_out, col_f, col_p,
    part, relay_l, relay_r, direct_l, direct_r, total, g_row, result, gw_sumup,
    gw_part, gw_core, gw_sum, gw_ring, gw_line, gw_last,
    own_sem, w_send, w_recv, o_send, o_recv, b_send, b_recv, c_send, c_recv,
    x_send, x_recv, z_send, z_recv, g_send, g_recv,
):
    y, zl, c, x, zh = coords()
    s, m = lax.axis_index("seq"), lax.axis_index("mp")
    m_far = x * 2 + 1 - zh
    factor = HEAD_WIDTH ** (-0.5)
    core = device(y, zl, 1 - c, x, zh)
    rings = [device((y + d) % 4, zl, c, x, zh) for d in (1, 2, 3)]
    x1, x2, x3 = (x + 1) % 4, (x + 2) % 4, (x + 3) % 4
    right = device(y, zl, c, x1, zh)
    left = device(y, zl, c, x3, zh)
    far = device(y, zl, c, x, 1 - zh)
    after, before = ((s + 1) % 32, m), ((s + 31) % 32, m)
    user = zl // 2
    at_home = user == zh
    away = jnp.logical_not(at_home)

    barrier = pltpu.get_barrier_semaphore()
    for target in (right, left, far):
        pl.semaphore_signal(barrier, inc=1, device_id=target, device_id_type=MESH)

    @pl.loop(1, 32)
    def _(i):
        peer = (s + i) % 32
        pl.semaphore_signal(barrier, inc=1, device_id=(peer, m), device_id_type=MESH)
        pl.semaphore_signal(barrier, inc=1, device_id=(peer, m_far), device_id_type=MESH)

    pl.semaphore_wait(barrier, 65)

    sends = []

    def go(src, dst, send, recv, target):
        copy = remote(src, dst, send, recv, target)
        copy.start()
        sends.append(copy)

    def slot(yy, b, cc):
        return wide(yy * 4 + b * 2 + cc, 128)

    def og_half(xx, half):
        return og_buf.at[pl.ds(384 * half, 384), wide(xx, 512)]

    def og_own(half):
        return og_ref.at[pl.ds(384 * half, 384)]

    local = []

    def keep(src, dst, sem):
        copy = pltpu.make_async_copy(src, dst, sem)
        copy.start()
        local.append(copy)

    side = jnp.where(at_home, 0, 1)
    w_here = w_buf.at[side, :, slot(y, zl % 2, c)]
    w_index = side * 2 + zl % 2
    for d in range(1, 4):
        go(w_ref, w_here, w_send.at[d], w_recv.at[w_index], device(y, (zl + d) % 4, c, x, user))
    w_away = remote(w_ref, w_here, w_send.at[0], w_recv.at[w_index], far)
    w_home = pltpu.make_async_copy(w_ref, w_here, w_recv.at[w_index])

    @pl.when(away)
    def _():
        w_away.start()

    @pl.when(at_home)
    def _():
        w_home.start()

    go(og_own(0), og_half(x, 0), o_send.at[0], o_recv.at[0], right)
    go(og_own(1), og_half(x, 1), o_send.at[1], o_recv.at[1], left)
    go(og_own(1), og_half(x, 1), o_send.at[2], o_recv.at[2], right)
    go(og_own(0), og_half(x, 0), o_send.at[3], o_recv.at[3], left)
    row_part, col_part = pl.ds(0, 256), pl.ds(256, 256)
    keep(q_ref.at[:, :, row_part], row_q, own_sem.at[0])
    keep(k_ref.at[:, :, row_part], row_k.at[pl.ds(1, 3)], own_sem.at[1])
    keep(v_ref.at[:, :, row_part], row_v.at[pl.ds(1, 3)], own_sem.at[2])
    keep(og_ref, og_buf.at[:, wide(x, 512)], own_sem.at[3])
    go(k_ref.at[2, :, row_part], row_k.at[0], b_send.at[0], b_recv.at[0], after)
    go(v_ref.at[2, :, row_part], row_v.at[0], b_send.at[1], b_recv.at[1], after)

    def spot(ref, owner):
        return ref.at[:, wide(owner // 2, 16), pl.ds(pl.multiple_of(256 + 128 * (owner % 2), 128), 128)]

    def to_columns(pairs, number):
        @pl.loop(1, 32)
        def _(i):
            peer = (s + i) % 32
            for src, dst in pairs:
                remote(
                    spot(src, peer), dst.at[pl.ds(3 * s, 3)], c_send.at[number], c_recv.at[number], (peer, m)
                ).start()

        for src, dst in pairs:
            pltpu.make_async_copy(spot(src, s), dst.at[pl.ds(3 * s, 3)], c_recv.at[number]).start()

    def to_far_columns(src, dst, number):
        @pl.loop(0, 32)
        def _(i):
            peer = (s + i) % 32
            remote(
                spot(src, peer), dst.at[pl.ds(3 * s, 3)], c_send.at[number], c_recv.at[number], (peer, m_far)
            ).start()

    def to_rows(pairs, number):
        @pl.loop(1, 32)
        def _(i):
            peer = (s + i) % 32
            for n, (src, dst) in enumerate(pairs):
                remote(
                    src.at[pl.ds(3 * peer, 3)], spot(dst, s), c_send.at[number + n], c_recv.at[number + n], (peer, m)
                ).start()

        for n, (src, dst) in enumerate(pairs):
            pltpu.make_async_copy(src.at[pl.ds(3 * s, 3)], spot(dst, s), c_recv.at[number + n]).start()

    def to_far_rows(src, dst, number):
        @pl.loop(0, 32)
        def _(i):
            peer = (s + i) % 32
            remote(
                src.at[pl.ds(3 * peer, 3)], spot(dst, s), c_send.at[number], c_recv.at[number], (peer, m_far)
            ).start()

    to_columns([(q_ref, col_in.at[0]), (k_ref, col_in.at[1]), (v_ref, col_in.at[2])], 0)

    seen = lax.broadcasted_iota(jnp.int32, (256, 256), 0) >= lax.broadcasted_iota(jnp.int32, (256, 256), 1)

    def head(h):
        return pl.ds(pl.multiple_of(128 * h, 128), 128)

    def row_forward(t, h):
        queries = row_q[t, :, head(h)]
        own = dot(queries, row_k[t + 1, :, head(h)], 1, 1)
        prior = dot(queries, row_k[t, :, head(h)], 1, 1)
        open_side = jnp.logical_or(t > 0, s > 0)
        prior = jnp.where(open_side, prior * factor, -1e30)
        scores = jnp.where(seen, own * factor, prior)
        weights = jnp.exp(scores - jnp.max(scores, axis=-1, keepdims=True))
        probs = (weights / jnp.sum(weights, axis=-1, keepdims=True)).astype(BF16)
        row_p[t, h] = probs
        zero = jnp.zeros_like(probs)
        outputs = dot(jnp.where(seen, probs, zero), row_v[t + 1, :, head(h)], 1, 0) + dot(
            jnp.where(seen, zero, probs), row_v[t, :, head(h)], 1, 0
        )
        mixed[t, :, head(h)] = outputs.astype(BF16)

    def row_backward(t, h):
        queries, probs, grads = row_q[t, :, head(h)], row_p[t, h], gm_row[t, :, head(h)]
        own = dot(grads, row_v[t + 1, :, head(h)], 1, 1)
        prior = dot(grads, row_v[t, :, head(h)], 1, 1)
        centre = jnp.sum(grads.astype(F32) * mixed[t, :, head(h)].astype(F32), axis=-1, keepdims=True)
        slopes = (probs.astype(F32) * (jnp.where(seen, own, prior) - centre)).astype(BF16)
        zero = jnp.zeros_like(probs)
        slopes_own, slopes_prior = jnp.where(seen, slopes, zero), jnp.where(seen, zero, slopes)
        probs_own, probs_prior = jnp.where(seen, probs, zero), jnp.where(seen, zero, probs)
        g_row[0, t, :, head(h)] = (
            (dot(slopes_own, row_k[t + 1, :, head(h)], 1, 0) + dot(slopes_prior, row_k[t, :, head(h)], 1, 0))
            * factor
        ).astype(BF16)
        gk_sum[t, :, head(h)] += dot(slopes_prior, queries, 0, 0)
        gv_sum[t, :, head(h)] += dot(probs_prior, grads, 0, 0)
        gk_sum[t + 1, :, head(h)] = dot(slopes_own, queries, 0, 0)
        gv_sum[t + 1, :, head(h)] = dot(probs_own, grads, 0, 0)

    below = lax.broadcasted_iota(jnp.int32, (96, 96), 0) >= lax.broadcasted_iota(jnp.int32, (96, 96), 1)

    def widen(src, dst):
        @pl.loop(0, 6)
        def _(i):
            dst[wide(i, 256), :] = src[wide(i, 16)].astype(F32).reshape(256, 128)

    def narrow(src, dst):
        @pl.loop(0, 6)
        def _(i):
            dst[wide(i, 16)] = src[wide(i, 256), :].astype(BF16).reshape(16, 16, 128)

    def column(j):
        return pl.ds(j, 96, stride=16)

    def col_forward(j):
        queries, keys, values = (col_f[a, column(j), :].astype(BF16) for a in range(3))
        scores = jnp.where(below, dot(queries, keys, 1, 1) * factor, -1e30)
        weights = jnp.exp(scores - jnp.max(scores, axis=-1, keepdims=True))
        probs = (weights / jnp.sum(weights, axis=-1, keepdims=True)).astype(BF16)
        col_p[j] = probs
        col_f[3, column(j), :] = dot(probs, values, 1, 0).astype(BF16).astype(F32)

    def col_backward(j):
        queries, keys, values = (col_f[a, column(j), :].astype(BF16) for a in range(3))
        outputs, wide_grads = col_f[3, column(j), :], col_f[4, column(j), :]
        probs, grads = col_p[j], wide_grads.astype(BF16)
        centre = jnp.sum(wide_grads * outputs, axis=-1, keepdims=True)
        slopes = (probs.astype(F32) * (dot(grads, values, 1, 1) - centre)).astype(BF16)
        col_f[0, column(j), :] = dot(slopes, keys, 1, 0) * factor
        col_f[1, column(j), :] = dot(slopes, queries, 0, 0) * factor
        col_f[2, column(j), :] = dot(probs, grads, 0, 0)

    def columns_of(body):
        @pl.loop(0, 2)
        def _(g):
            for b in range(8):
                body(8 * g + b)

    top, low = pl.ds(0, 384), pl.ds(384, 384)

    def project(xx):
        columns = wide(xx, 512)

        @pl.loop(0, 3)
        def _(t):
            part[wide(t, 256), columns] = (
                dot(mixed[t], w_buf[0, :, columns], 1, 0) + dot(mixed_far[t], w_buf[1, :, columns], 1, 0)
            ).astype(BF16)

    for copy in local[:3]:
        copy.wait()

    @pl.loop(2, 6)
    def _(u):
        row_forward(u // 2, u % 2)

    arrive(og_half(x3, 0), o_recv.at[0])
    go(og_half(x3, 0), og_half(x3, 0), o_send.at[4], o_recv.at[4], right)
    arrive(og_half(x1, 1), o_recv.at[1])
    go(og_half(x1, 1), og_half(x1, 1), o_send.at[5], o_recv.at[5], left)
    for b in range(2):
        for a in range(2):
            arrive(w_buf.at[a, :, slot(y, b, c)], w_recv.at[2 * a + b])
        block = w_buf.at[:, :, slot(y, b, c)]
        for d in range(2):
            go(block, block, w_send.at[4 + 2 * d + b], w_recv.at[4 + 2 * d + b], rings[2 * d])
        go(block, block, w_send.at[10 + b], w_recv.at[10 + b], core)
    for b in range(2):
        arrive((row_k, row_v)[b].at[0], b_recv.at[b])

    @pl.loop(0, 2)
    def _(h):
        row_forward(0, h)
    y1, y2, y3 = (y + 1) % 4, (y + 2) % 4, (y + 3) % 4

    def w_ring(yy, b, index, relay=None):
        block = w_buf.at[:, :, slot(yy, b, c)]
        arrive(block, w_recv.at[index])
        if relay is not None:
            go(block, block, w_send.at[8 + b], w_recv.at[8 + b], relay)
        go(block, block, w_send.at[8 + index], w_recv.at[8 + index], core)

    w_ring(y3, 0, 4, rings[0])
    w_ring(y1, 1, 7, rings[2])
    w_ring(y3, 1, 5)
    w_ring(y1, 0, 6)
    arrive(col_in, c_recv.at[0])
    go(mixed.at[:, :, row_part], mixed_far.at[:, :, row_part], z_send.at[0], z_recv.at[0], far)
    for a in range(3):
        widen(col_in.at[a], col_f.at[a])
    columns_of(col_forward)
    narrow(col_f.at[3], col_out.at[0])
    to_rows([(col_out.at[0], mixed)], 1)
    to_far_rows(col_out.at[0], mixed_far, 6)
    w_ring(y2, 0, 8)
    w_ring(y2, 1, 9)
    local[3].wait()
    arrive(og_half(x3, 1), o_recv.at[2])
    arrive(og_half(x1, 0), o_recv.at[3])
    arrive(og_half(x2, 0), o_recv.at[4])
    arrive(og_half(x2, 1), o_recv.at[5])
    for b in range(2):
        arrive(w_buf.at[:, :, slot(y, b, 1 - c)], w_recv.at[10 + b])
    for d in range(3):
        for b in range(2):
            arrive(w_buf.at[:, :, slot((y3, y1, y2)[d], b, 1 - c)], w_recv.at[12 + 2 * d + b])

    @pl.loop(0, 3)
    def _(t):
        gm_far[t] = dot(og_buf[wide(t, 256), :], w_buf[1], 1, 1).astype(BF16)

    to_far_columns(gm_far, col_gm.at[1], 7)

    @pl.loop(0, 3)
    def _(t):
        value = dot(og_buf[wide(t, 256), :], w_buf[0], 1, 1)
        total[t] = value
        gm_own[t] = value.astype(BF16)

    to_columns([(gm_own, col_gm.at[0])], 2)

    arrive(mixed_far.at[:, :, row_part], z_recv.at[0])
    arrive(mixed.at[:, :, col_part], c_recv.at[1])
    arrive(mixed_far.at[:, :, col_part], c_recv.at[6])
    project(x2)
    go(part.at[top, wide(x2, 512)], relay_l, x_send.at[0], x_recv.at[0], right)
    go(part.at[low, wide(x2, 512)], relay_r, x_send.at[1], x_recv.at[1], left)
    project(x1)
    go(part.at[low, wide(x1, 512)], direct_l.at[low], x_send.at[2], x_recv.at[2], right)
    project(x3)
    go(part.at[top, wide(x3, 512)], direct_r.at[top], x_send.at[3], x_recv.at[3], left)

    for a, ref in enumerate((mixed, mixed_far)):
        for group in range(4):

            @pl.loop(0, 2)
            def _(tile):
                rows = wide(tile, 256)
                value = jnp.zeros((256, 512), F32)
                for t in range(3):
                    value += dot(ref[t, :, rows], og_buf[pl.ds(256 * t, 256), pl.ds(512 * group, 512)], 0, 0)
                value = value.astype(BF16)
                for j in range(4):
                    gw_part[j % 2, group, j // 2, a, rows, :] = value[:, 128 * j : 128 * j + 128]

    go(gw_part.at[1 - c], gw_core, g_send.at[0], g_recv.at[0], core)
    arrive(col_gm.at[0], c_send.at[7])
    go(gm_far.at[:, :, row_part], gm_in, z_send.at[1], z_recv.at[1], far)
    arrive(relay_l, x_recv.at[0])
    part[top, wide(x1, 512)] = (part[top, wide(x1, 512)].astype(F32) + relay_l[...].astype(F32)).astype(BF16)
    go(part.at[top, wide(x1, 512)], direct_l.at[top], x_send.at[4], x_recv.at[4], right)
    arrive(relay_r, x_recv.at[1])
    part[low, wide(x3, 512)] = (part[low, wide(x3, 512)].astype(F32) + relay_r[...].astype(F32)).astype(BF16)
    go(part.at[low, wide(x3, 512)], direct_r.at[low], x_send.at[5], x_recv.at[5], left)

    arrive(gw_core, g_recv.at[0])
    for b in range(2):
        for d in (2, 1, 3, 0):
            yy = (y + d) % 4
            gw_sum[yy, b] = (gw_part[c, yy, b].astype(F32) + gw_core[yy, b].astype(F32)).astype(BF16)
            if d:
                index = 2 * d - 1 + b
                go(gw_sum.at[yy, b], gw_ring.at[d - 1, b], g_send.at[index], g_recv.at[index], rings[d - 1])

    arrive(col_gm.at[0], c_recv.at[2])
    arrive(col_gm.at[1], c_recv.at[7])

    @pl.loop(0, 6)
    def _(i):
        rows = wide(i, 16)
        value = (col_gm[0, rows].astype(F32) + col_gm[1, rows].astype(F32)).astype(BF16)
        col_f[4, wide(i, 256), :] = value.astype(F32).reshape(256, 128)

    columns_of(col_backward)
    for a in range(3):
        narrow(col_f.at[a], col_out.at[a + 1])
    to_rows([(col_out.at[1], gq_ref), (col_out.at[2], gk_ref), (col_out.at[3], gv_ref)], 3)

    ends = []
    def end(b):
        for d in range(3):
            arrive(gw_ring.at[d, b], g_recv.at[2 * d + 1 + b])
        gw_line[b] = (
            gw_sum[y, b].astype(F32)
            + gw_ring[0, b].astype(F32)
            + gw_ring[1, b].astype(F32)
            + gw_ring[2, b].astype(F32)
        ).astype(BF16)
        away_copy = remote(
            gw_line.at[b, 1], gw_last.at[zl], g_send.at[7 + b], g_recv.at[7 + zl], device(y, 2 * zh + b, c, x, 1 - zh)
        )
        away_copy.start()
        sends.append(away_copy)
        other = zl != 2 * zh + b
        copy = remote(
            gw_line.at[b, 0], gw_last.at[zl], g_send.at[9 + b], g_recv.at[7 + zl], device(y, 2 * zh + b, c, x, zh)
        )
        home = pltpu.make_async_copy(gw_line.at[b, 0], gw_last.at[zl], g_recv.at[7 + zl])

        @pl.when(other)
        def _():
            copy.start()

        @pl.when(jnp.logical_not(other))
        def _():
            home.start()

        ends.append((other, copy))

    arrive(gm_in, z_recv.at[1])

    @pl.loop(0, 3)
    def _(t):
        gm_row[t] = (total[t, :, row_part] + gm_in[t].astype(F32)).astype(BF16)

    gk_sum[0] = jnp.zeros_like(gk_sum[0])
    gv_sum[0] = jnp.zeros_like(gv_sum[0])

    @pl.loop(0, 2)
    def _(h):
        row_backward(0, h)

    edge_out[0] = (gk_sum[0] * factor).astype(BF16)
    edge_out[1] = gv_sum[0].astype(BF16)
    go(edge_out, edge_in, b_send.at[2], b_recv.at[2], before)
    end(0)
    end(1)

    @pl.loop(2, 6)
    def _(u):
        row_backward(u // 2, u % 2)

    keep(g_row.at[0], gq_ref.at[:, :, row_part], own_sem.at[4])

    project(x)
    arrive(direct_l.at[low], x_recv.at[2])
    arrive(direct_r.at[top], x_recv.at[3])
    arrive(direct_l.at[top], x_recv.at[4])
    arrive(direct_r.at[low], x_recv.at[5])

    @pl.loop(0, 3)
    def _(t):
        rows = wide(t, 256)
        result[t] = (
            part[rows, wide(x, 512)].astype(F32) + direct_l[rows].astype(F32) + direct_r[rows].astype(F32)
        ).astype(BF16)

    keep(result, out_ref, own_sem.at[5])
    arrive(edge_in, b_recv.at[2])

    @pl.loop(0, 3)
    def _(t):
        edge_k = jnp.where(t == 2, edge_in[0].astype(F32), 0.0)
        edge_v = jnp.where(t == 2, edge_in[1].astype(F32), 0.0)
        g_row[1, t] = (gk_sum[t + 1] * factor + edge_k).astype(BF16)
        g_row[2, t] = (gv_sum[t + 1] + edge_v).astype(BF16)

    keep(g_row.at[1], gk_ref.at[:, :, row_part], own_sem.at[6])
    keep(g_row.at[2], gv_ref.at[:, :, row_part], own_sem.at[7])

    for n, ref in enumerate((gq_ref, gk_ref, gv_ref)):
        arrive(ref.at[:, :, col_part], c_recv.at[3 + n])
    for z in range(4):
        arrive(gw_last.at[z], g_recv.at[7 + z])
    gw_sumup[...] = (
        gw_last[0].astype(F32) + gw_last[1].astype(F32) + gw_last[2].astype(F32) + gw_last[3].astype(F32)
    ).astype(BF16)
    keep(gw_sumup, gw_ref, own_sem.at[8])
    arrive(col_in.at[:, pl.ds(0, 93)], c_send.at[0])
    arrive(col_out.at[0, pl.ds(0, 93)], c_send.at[1])
    arrive(col_gm.at[0, pl.ds(0, 93)], c_send.at[2])
    for n in range(3):
        arrive(col_out.at[n + 1, pl.ds(0, 93)], c_send.at[3 + n])
    arrive(col_out.at[0], c_send.at[6])
    for copy in local[4:]:
        copy.wait()
    for copy in sends:
        copy.wait_send()
    for other, copy in ends:

        @pl.when(other)
        def _():
            copy.wait_send()

    @pl.when(away)
    def _():
        w_away.wait_send()


def hand_over(*refs):
    sources, targets, buffers, in_sem, out_sem = refs[:5], refs[5:10], refs[10:15], refs[15], refs[16]
    loads = [pltpu.make_async_copy(sources[n], buffers[n], in_sem.at[n]) for n in range(5)]
    stores = [pltpu.make_async_copy(buffers[n], targets[n], out_sem.at[n]) for n in range(5)]
    for copy in loads:
        copy.start()
    for load, store in zip(loads, stores):
        load.wait()
        store.start()
    for copy in stores:
        copy.wait()


def per_device(query, key, value, weight_out, output_gradient):
    rows = jax.ShapeDtypeStruct((3, 256, 512), BF16)
    flat = jax.ShapeDtypeStruct((768, 512), BF16)
    any_space = pl.BlockSpec(memory_space=pl.ANY)
    dma = pltpu.SemaphoreType.DMA

    def half(*shape):
        return pltpu.VMEM(shape, BF16)

    def full(*shape):
        return pltpu.VMEM(shape, F32)

    results = pl.pallas_call(
        layer_kernel,
        out_shape=(rows, rows, rows, rows, jax.ShapeDtypeStruct((512, 128), BF16)),
        in_specs=[any_space] * 5,
        out_specs=(any_space,) * 5,
        scratch_shapes=[
            half(2, 512, 2048),
            half(768, 2048),
            half(3, 256, 256),
            half(4, 256, 256),
            half(4, 256, 256),
            half(3, 2, 256, 256),
            half(3, 256, 512),
            half(3, 256, 512),
            half(3, 256, 256),
            half(3, 256, 256),
            half(3, 256, 512),
            half(3, 256, 512),
            full(4, 256, 256),
            full(4, 256, 256),
            half(2, 256, 256),
            half(2, 256, 256),
            half(3, 96, 16, 128),
            half(2, 96, 16, 128),
            half(4, 96, 16, 128),
            full(5, 1536, 128),
            half(16, 96, 96),
            half(768, 2048),
            half(384, 512),
            half(384, 512),
            half(768, 512),
            half(768, 512),
            full(3, 256, 512),
            half(3, 3, 256, 256),
            half(3, 256, 512),
            half(512, 128),
            half(2, 4, 2, 2, 512, 128),
            half(4, 2, 2, 512, 128),
            half(4, 2, 2, 512, 128),
            half(3, 2, 2, 512, 128),
            half(2, 2, 512, 128),
            half(4, 512, 128),
            dma((9,)),
            dma((18,)),
            dma((18,)),
            dma((6,)),
            dma((6,)),
            dma((3,)),
            dma((3,)),
            dma((8,)),
            dma((8,)),
            dma((6,)),
            dma((6,)),
            dma((2,)),
            dma((2,)),
            dma((11,)),
            dma((11,)),
        ],
        compiler_params=pltpu.CompilerParams(
            collective_id=0, has_side_effects=True, vmem_limit_bytes=62 * 2**20
        ),
    )(
        query.reshape(3, 256, 512),
        key.reshape(3, 256, 512),
        value.reshape(3, 256, 512),
        weight_out,
        output_gradient,
    )
    return pl.pallas_call(
        hand_over,
        out_shape=(flat, flat, flat, flat, jax.ShapeDtypeStruct((512, 128), BF16)),
        in_specs=[any_space] * 5,
        out_specs=(any_space,) * 5,
        scratch_shapes=[half(768, 512)] * 4 + [half(512, 128), dma((5,)), dma((5,))],
    )(*(array.reshape(-1, array.shape[-1]) for array in results))


def solution(mesh):
    in_specs = (P("seq", "mp"), P("seq", "mp"), P("seq", "mp"), P("mp", "seq"), P("seq", "mp"))
    out_specs = (P("seq", "mp"), P("seq", "mp"), P("seq", "mp"), P("seq", "mp"), P("mp", "seq"))
    return jax.shard_map(
        per_device, mesh=mesh, in_specs=in_specs, out_specs=out_specs, check_vma=False
    )
```

```python
import jax
import jax.numpy as jnp
from jax import lax
from jax.experimental import pallas as pl
from jax.experimental.pallas import tpu as pltpu
from jax.sharding import PartitionSpec as P

HEAD_WIDTH = 128
ROW_LENGTH = 256
MESH = pl.DeviceIdType.MESH
F32 = jnp.float32
BF16 = jnp.bfloat16


def coords():
    s = lax.axis_index("seq")
    m = lax.axis_index("mp")
    return s // 8, (s // 2) % 4, s % 2, m // 2, m % 2


def device(y, zl, c, x, zh):
    return (y * 8 + zl * 2 + c, x * 2 + zh)


def remote(src, dst, send, recv, target):
    return pltpu.make_async_remote_copy(
        src_ref=src, dst_ref=dst, send_sem=send, recv_sem=recv, device_id=target, device_id_type=MESH
    )


def arrive(ref, sem):
    pltpu.make_async_copy(ref, ref, sem).wait()


def wide(index, width):
    return pl.ds(pl.multiple_of(index * width, width), width)


def dot(a, b, left, right):
    return lax.dot_general(a, b, (((left,), (right,)), ((), ())), preferred_element_type=F32)


def layer_kernel(
    q_ref, k_ref, v_ref, w_ref, og_ref,
    out_ref, gq_ref, gk_ref, gv_ref, gw_ref,
    w_buf, og_buf, row_q, row_k, row_v, row_p, gm_own, gm_far, gm_row, gm_in, mixed, mixed_far,
    gk_sum, gv_sum, edge_out, edge_in,
    col_in, col_gm, col_out, col_f, col_p,
    part, relay_l, relay_r, direct_l, direct_r, total, g_row, result, gw_sumup,
    gw_part, gw_core, gw_sum, gw_ring, gw_line, gw_last,
    own_sem, w_send, w_recv, o_send, o_recv, b_send, b_recv, c_send, c_recv,
    x_send, x_recv, z_send, z_recv, g_send, g_recv,
):
    y, zl, c, x, zh = coords()
    s, m = lax.axis_index("seq"), lax.axis_index("mp")
    m_far = x * 2 + 1 - zh
    factor = HEAD_WIDTH ** (-0.5)
    core = device(y, zl, 1 - c, x, zh)
    rings = [device((y + d) % 4, zl, c, x, zh) for d in (1, 2, 3)]
    x1, x2, x3 = (x + 1) % 4, (x + 2) % 4, (x + 3) % 4
    right = device(y, zl, c, x1, zh)
    left = device(y, zl, c, x3, zh)
    far = device(y, zl, c, x, 1 - zh)
    after, before = ((s + 1) % 32, m), ((s + 31) % 32, m)
    user = zl // 2
    at_home = user == zh
    away = jnp.logical_not(at_home)

    barrier = pltpu.get_barrier_semaphore()
    for target in (right, left, far):
        pl.semaphore_signal(barrier, inc=1, device_id=target, device_id_type=MESH)

    @pl.loop(1, 32)
    def _(i):
        peer = (s + i) % 32
        pl.semaphore_signal(barrier, inc=1, device_id=(peer, m), device_id_type=MESH)
        pl.semaphore_signal(barrier, inc=1, device_id=(peer, m_far), device_id_type=MESH)

    pl.semaphore_wait(barrier, 65)

    sends = []

    def go(src, dst, send, recv, target):
        copy = remote(src, dst, send, recv, target)
        copy.start()
        sends.append(copy)

    def slot(yy, b, cc):
        return wide(yy * 4 + b * 2 + cc, 128)

    def og_half(xx, half):
        return og_buf.at[pl.ds(384 * half, 384), wide(xx, 512)]

    def og_own(half):
        return og_ref.at[pl.ds(384 * half, 384)]

    local = []

    def keep(src, dst, sem):
        copy = pltpu.make_async_copy(src, dst, sem)
        copy.start()
        local.append(copy)

    side = jnp.where(at_home, 0, 1)
    w_here = w_buf.at[side, :, slot(y, zl % 2, c)]
    w_index = side * 2 + zl % 2
    for d in range(1, 4):
        go(w_ref, w_here, w_send.at[d], w_recv.at[w_index], device(y, (zl + d) % 4, c, x, user))
    w_away = remote(w_ref, w_here, w_send.at[0], w_recv.at[w_index], far)
    w_home = pltpu.make_async_copy(w_ref, w_here, w_recv.at[w_index])

    @pl.when(away)
    def _():
        w_away.start()

    @pl.when(at_home)
    def _():
        w_home.start()

    go(og_own(0), og_half(x, 0), o_send.at[0], o_recv.at[0], right)
    go(og_own(1), og_half(x, 1), o_send.at[1], o_recv.at[1], left)
    go(og_own(1), og_half(x, 1), o_send.at[2], o_recv.at[2], right)
    go(og_own(0), og_half(x, 0), o_send.at[3], o_recv.at[3], left)
    row_part, col_part = pl.ds(0, 256), pl.ds(256, 256)
    keep(q_ref.at[:, :, row_part], row_q, own_sem.at[0])
    keep(k_ref.at[:, :, row_part], row_k.at[pl.ds(1, 3)], own_sem.at[1])
    keep(v_ref.at[:, :, row_part], row_v.at[pl.ds(1, 3)], own_sem.at[2])
    keep(og_ref, og_buf.at[:, wide(x, 512)], own_sem.at[3])
    go(k_ref.at[2, :, row_part], row_k.at[0], b_send.at[0], b_recv.at[0], after)
    go(v_ref.at[2, :, row_part], row_v.at[0], b_send.at[1], b_recv.at[1], after)

    def spot(ref, owner):
        return ref.at[:, wide(owner // 2, 16), pl.ds(pl.multiple_of(256 + 128 * (owner % 2), 128), 128)]

    def to_columns(pairs, number):
        @pl.loop(1, 32)
        def _(i):
            peer = (s + i) % 32
            for src, dst in pairs:
                remote(
                    spot(src, peer), dst.at[pl.ds(3 * s, 3)], c_send.at[number], c_recv.at[number], (peer, m)
                ).start()

        for src, dst in pairs:
            pltpu.make_async_copy(spot(src, s), dst.at[pl.ds(3 * s, 3)], c_recv.at[number]).start()

    def to_far_columns(src, dst, number):
        @pl.loop(0, 32)
        def _(i):
            peer = (s + i) % 32
            remote(
                spot(src, peer), dst.at[pl.ds(3 * s, 3)], c_send.at[number], c_recv.at[number], (peer, m_far)
            ).start()

    def to_rows(pairs, number):
        @pl.loop(1, 32)
        def _(i):
            peer = (s + i) % 32
            for n, (src, dst) in enumerate(pairs):
                remote(
                    src.at[pl.ds(3 * peer, 3)], spot(dst, s), c_send.at[number + n], c_recv.at[number + n], (peer, m)
                ).start()

        for n, (src, dst) in enumerate(pairs):
            pltpu.make_async_copy(src.at[pl.ds(3 * s, 3)], spot(dst, s), c_recv.at[number + n]).start()

    def to_far_rows(src, dst, number):
        @pl.loop(0, 32)
        def _(i):
            peer = (s + i) % 32
            remote(
                src.at[pl.ds(3 * peer, 3)], spot(dst, s), c_send.at[number], c_recv.at[number], (peer, m_far)
            ).start()

    to_columns([(q_ref, col_in.at[0]), (k_ref, col_in.at[1]), (v_ref, col_in.at[2])], 0)

    seen = lax.broadcasted_iota(jnp.int32, (256, 256), 0) >= lax.broadcasted_iota(jnp.int32, (256, 256), 1)

    def head(h):
        return pl.ds(pl.multiple_of(128 * h, 128), 128)

    def row_forward(t, h):
        queries = row_q[t, :, head(h)]
        own = dot(queries, row_k[t + 1, :, head(h)], 1, 1)
        prior = dot(queries, row_k[t, :, head(h)], 1, 1)
        open_side = jnp.logical_or(t > 0, s > 0)
        prior = jnp.where(open_side, prior * factor, -1e30)
        scores = jnp.where(seen, own * factor, prior)
        weights = jnp.exp(scores - jnp.max(scores, axis=-1, keepdims=True))
        probs = (weights / jnp.sum(weights, axis=-1, keepdims=True)).astype(BF16)
        row_p[t, h] = probs
        zero = jnp.zeros_like(probs)
        outputs = dot(jnp.where(seen, probs, zero), row_v[t + 1, :, head(h)], 1, 0) + dot(
            jnp.where(seen, zero, probs), row_v[t, :, head(h)], 1, 0
        )
        mixed[t, :, head(h)] = outputs.astype(BF16)

    def row_backward(t, h):
        queries, probs, grads = row_q[t, :, head(h)], row_p[t, h], gm_row[t, :, head(h)]
        own = dot(grads, row_v[t + 1, :, head(h)], 1, 1)
        prior = dot(grads, row_v[t, :, head(h)], 1, 1)
        centre = jnp.sum(grads.astype(F32) * mixed[t, :, head(h)].astype(F32), axis=-1, keepdims=True)
        slopes = (probs.astype(F32) * (jnp.where(seen, own, prior) - centre)).astype(BF16)
        zero = jnp.zeros_like(probs)
        slopes_own, slopes_prior = jnp.where(seen, slopes, zero), jnp.where(seen, zero, slopes)
        probs_own, probs_prior = jnp.where(seen, probs, zero), jnp.where(seen, zero, probs)
        g_row[0, t, :, head(h)] = (
            (dot(slopes_own, row_k[t + 1, :, head(h)], 1, 0) + dot(slopes_prior, row_k[t, :, head(h)], 1, 0))
            * factor
        ).astype(BF16)
        gk_sum[t, :, head(h)] += dot(slopes_prior, queries, 0, 0)
        gv_sum[t, :, head(h)] += dot(probs_prior, grads, 0, 0)
        gk_sum[t + 1, :, head(h)] = dot(slopes_own, queries, 0, 0)
        gv_sum[t + 1, :, head(h)] = dot(probs_own, grads, 0, 0)

    below = lax.broadcasted_iota(jnp.int32, (96, 96), 0) >= lax.broadcasted_iota(jnp.int32, (96, 96), 1)

    def widen(src, dst):
        @pl.loop(0, 6)
        def _(i):
            dst[wide(i, 256), :] = src[wide(i, 16)].astype(F32).reshape(256, 128)

    def narrow(src, dst):
        @pl.loop(0, 6)
        def _(i):
            dst[wide(i, 16)] = src[wide(i, 256), :].astype(BF16).reshape(16, 16, 128)

    def column(j):
        return pl.ds(j, 96, stride=16)

    def col_forward(j):
        queries, keys, values = (col_f[a, column(j), :].astype(BF16) for a in range(3))
        scores = jnp.where(below, dot(queries, keys, 1, 1) * factor, -1e30)
        weights = jnp.exp(scores - jnp.max(scores, axis=-1, keepdims=True))
        probs = (weights / jnp.sum(weights, axis=-1, keepdims=True)).astype(BF16)
        col_p[j] = probs
        col_f[3, column(j), :] = dot(probs, values, 1, 0).astype(BF16).astype(F32)

    def col_backward(j):
        queries, keys, values = (col_f[a, column(j), :].astype(BF16) for a in range(3))
        outputs, wide_grads = col_f[3, column(j), :], col_f[4, column(j), :]
        probs, grads = col_p[j], wide_grads.astype(BF16)
        centre = jnp.sum(wide_grads * outputs, axis=-1, keepdims=True)
        slopes = (probs.astype(F32) * (dot(grads, values, 1, 1) - centre)).astype(BF16)
        col_f[0, column(j), :] = dot(slopes, keys, 1, 0) * factor
        col_f[1, column(j), :] = dot(slopes, queries, 0, 0) * factor
        col_f[2, column(j), :] = dot(probs, grads, 0, 0)

    def columns_of(body):
        @pl.loop(0, 2)
        def _(g):
            for b in range(8):
                body(8 * g + b)

    top, low = pl.ds(0, 384), pl.ds(384, 384)

    def project(xx):
        columns = wide(xx, 512)

        @pl.loop(0, 3)
        def _(t):
            part[wide(t, 256), columns] = (
                dot(mixed[t], w_buf[0, :, columns], 1, 0) + dot(mixed_far[t], w_buf[1, :, columns], 1, 0)
            ).astype(BF16)

    for copy in local[:3]:
        copy.wait()

    @pl.loop(2, 6)
    def _(u):
        row_forward(u // 2, u % 2)

    arrive(og_half(x3, 0), o_recv.at[0])
    go(og_half(x3, 0), og_half(x3, 0), o_send.at[4], o_recv.at[4], right)
    arrive(og_half(x1, 1), o_recv.at[1])
    go(og_half(x1, 1), og_half(x1, 1), o_send.at[5], o_recv.at[5], left)
    for b in range(2):
        for a in range(2):
            arrive(w_buf.at[a, :, slot(y, b, c)], w_recv.at[2 * a + b])
        block = w_buf.at[:, :, slot(y, b, c)]
        for d in range(2):
            go(block, block, w_send.at[4 + 2 * d + b], w_recv.at[4 + 2 * d + b], rings[2 * d])
        go(block, block, w_send.at[10 + b], w_recv.at[10 + b], core)
    for b in range(2):
        arrive((row_k, row_v)[b].at[0], b_recv.at[b])

    @pl.loop(0, 2)
    def _(h):
        row_forward(0, h)
    y1, y2, y3 = (y + 1) % 4, (y + 2) % 4, (y + 3) % 4

    def w_ring(yy, b, index, relay=None):
        block = w_buf.at[:, :, slot(yy, b, c)]
        arrive(block, w_recv.at[index])
        if relay is not None:
            go(block, block, w_send.at[8 + b], w_recv.at[8 + b], relay)
        go(block, block, w_send.at[8 + index], w_recv.at[8 + index], core)

    w_ring(y3, 0, 4, rings[0])
    w_ring(y1, 1, 7, rings[2])
    w_ring(y3, 1, 5)
    w_ring(y1, 0, 6)
    arrive(col_in, c_recv.at[0])
    go(mixed.at[:, :, row_part], mixed_far.at[:, :, row_part], z_send.at[0], z_recv.at[0], far)
    for a in range(3):
        widen(col_in.at[a], col_f.at[a])
    columns_of(col_forward)
    narrow(col_f.at[3], col_out.at[0])
    to_rows([(col_out.at[0], mixed)], 1)
    to_far_rows(col_out.at[0], mixed_far, 6)
    w_ring(y2, 0, 8)
    w_ring(y2, 1, 9)
    local[3].wait()
    arrive(og_half(x3, 1), o_recv.at[2])
    arrive(og_half(x1, 0), o_recv.at[3])
    arrive(og_half(x2, 0), o_recv.at[4])
    arrive(og_half(x2, 1), o_recv.at[5])
    for b in range(2):
        arrive(w_buf.at[:, :, slot(y, b, 1 - c)], w_recv.at[10 + b])
    for d in range(3):
        for b in range(2):
            arrive(w_buf.at[:, :, slot((y3, y1, y2)[d], b, 1 - c)], w_recv.at[12 + 2 * d + b])

    @pl.loop(0, 3)
    def _(t):
        gm_far[t] = dot(og_buf[wide(t, 256), :], w_buf[1], 1, 1).astype(BF16)

    to_far_columns(gm_far, col_gm.at[1], 7)

    @pl.loop(0, 3)
    def _(t):
        value = dot(og_buf[wide(t, 256), :], w_buf[0], 1, 1)
        total[t] = value
        gm_own[t] = value.astype(BF16)

    to_columns([(gm_own, col_gm.at[0])], 2)

    arrive(mixed_far.at[:, :, row_part], z_recv.at[0])
    arrive(mixed.at[:, :, col_part], c_recv.at[1])
    arrive(mixed_far.at[:, :, col_part], c_recv.at[6])
    project(x2)
    go(part.at[top, wide(x2, 512)], relay_l, x_send.at[0], x_recv.at[0], right)
    go(part.at[low, wide(x2, 512)], relay_r, x_send.at[1], x_recv.at[1], left)
    project(x1)
    go(part.at[low, wide(x1, 512)], direct_l.at[low], x_send.at[2], x_recv.at[2], right)
    project(x3)
    go(part.at[top, wide(x3, 512)], direct_r.at[top], x_send.at[3], x_recv.at[3], left)

    for a, ref in enumerate((mixed, mixed_far)):
        for group in range(4):

            @pl.loop(0, 2)
            def _(tile):
                rows = wide(tile, 256)
                value = jnp.zeros((256, 512), F32)
                for t in range(3):
                    value += dot(ref[t, :, rows], og_buf[pl.ds(256 * t, 256), pl.ds(512 * group, 512)], 0, 0)
                value = value.astype(BF16)
                for j in range(4):
                    gw_part[j % 2, group, j // 2, a, rows, :] = value[:, 128 * j : 128 * j + 128]

    go(gw_part.at[1 - c], gw_core, g_send.at[0], g_recv.at[0], core)
    arrive(col_gm.at[0], c_send.at[7])
    go(gm_far.at[:, :, row_part], gm_in, z_send.at[1], z_recv.at[1], far)
    arrive(relay_l, x_recv.at[0])
    part[top, wide(x1, 512)] = (part[top, wide(x1, 512)].astype(F32) + relay_l[...].astype(F32)).astype(BF16)
    go(part.at[top, wide(x1, 512)], direct_l.at[top], x_send.at[4], x_recv.at[4], right)
    arrive(relay_r, x_recv.at[1])
    part[low, wide(x3, 512)] = (part[low, wide(x3, 512)].astype(F32) + relay_r[...].astype(F32)).astype(BF16)
    go(part.at[low, wide(x3, 512)], direct_r.at[low], x_send.at[5], x_recv.at[5], left)

    arrive(gw_core, g_recv.at[0])
    for b in range(2):
        for d in (2, 1, 3, 0):
            yy = (y + d) % 4
            gw_sum[yy, b] = (gw_part[c, yy, b].astype(F32) + gw_core[yy, b].astype(F32)).astype(BF16)
            if d:
                index = 2 * d - 1 + b
                go(gw_sum.at[yy, b], gw_ring.at[d - 1, b], g_send.at[index], g_recv.at[index], rings[d - 1])

    arrive(col_gm.at[0], c_recv.at[2])
    arrive(col_gm.at[1], c_recv.at[7])

    @pl.loop(0, 6)
    def _(i):
        rows = wide(i, 16)
        value = (col_gm[0, rows].astype(F32) + col_gm[1, rows].astype(F32)).astype(BF16)
        col_f[4, wide(i, 256), :] = value.astype(F32).reshape(256, 128)

    columns_of(col_backward)
    for a in range(3):
        narrow(col_f.at[a], col_out.at[a + 1])
    to_rows([(col_out.at[1], gq_ref), (col_out.at[2], gk_ref), (col_out.at[3], gv_ref)], 3)

    ends = []
    def end(b):
        for d in range(3):
            arrive(gw_ring.at[d, b], g_recv.at[2 * d + 1 + b])
        gw_line[b] = (
            gw_sum[y, b].astype(F32)
            + gw_ring[0, b].astype(F32)
            + gw_ring[1, b].astype(F32)
            + gw_ring[2, b].astype(F32)
        ).astype(BF16)
        away_copy = remote(
            gw_line.at[b, 1], gw_last.at[zl], g_send.at[7 + b], g_recv.at[7 + zl], device(y, 2 * zh + b, c, x, 1 - zh)
        )
        away_copy.start()
        sends.append(away_copy)
        other = zl != 2 * zh + b
        copy = remote(
            gw_line.at[b, 0], gw_last.at[zl], g_send.at[9 + b], g_recv.at[7 + zl], device(y, 2 * zh + b, c, x, zh)
        )
        home = pltpu.make_async_copy(gw_line.at[b, 0], gw_last.at[zl], g_recv.at[7 + zl])

        @pl.when(other)
        def _():
            copy.start()

        @pl.when(jnp.logical_not(other))
        def _():
            home.start()

        ends.append((other, copy))

    arrive(gm_in, z_recv.at[1])

    @pl.loop(0, 3)
    def _(t):
        gm_row[t] = (total[t, :, row_part] + gm_in[t].astype(F32)).astype(BF16)

    gk_sum[0] = jnp.zeros_like(gk_sum[0])
    gv_sum[0] = jnp.zeros_like(gv_sum[0])

    @pl.loop(0, 2)
    def _(h):
        row_backward(0, h)

    edge_out[0] = (gk_sum[0] * factor).astype(BF16)
    edge_out[1] = gv_sum[0].astype(BF16)
    go(edge_out, edge_in, b_send.at[2], b_recv.at[2], before)
    end(0)
    end(1)

    @pl.loop(2, 6)
    def _(u):
        row_backward(u // 2, u % 2)

    keep(g_row.at[0], gq_ref.at[:, :, row_part], own_sem.at[4])

    project(x)
    arrive(direct_l.at[low], x_recv.at[2])
    arrive(direct_r.at[top], x_recv.at[3])
    arrive(direct_l.at[top], x_recv.at[4])
    arrive(direct_r.at[low], x_recv.at[5])

    @pl.loop(0, 3)
    def _(t):
        rows = wide(t, 256)
        result[t] = (
            part[rows, wide(x, 512)].astype(F32) + direct_l[rows].astype(F32) + direct_r[rows].astype(F32)
        ).astype(BF16)

    keep(result, out_ref, own_sem.at[5])
    arrive(edge_in, b_recv.at[2])

    @pl.loop(0, 3)
    def _(t):
        edge_k = jnp.where(t == 2, edge_in[0].astype(F32), 0.0)
        edge_v = jnp.where(t == 2, edge_in[1].astype(F32), 0.0)
        g_row[1, t] = (gk_sum[t + 1] * factor + edge_k).astype(BF16)
        g_row[2, t] = (gv_sum[t + 1] + edge_v).astype(BF16)

    keep(g_row.at[1], gk_ref.at[:, :, row_part], own_sem.at[6])
    keep(g_row.at[2], gv_ref.at[:, :, row_part], own_sem.at[7])

    for n, ref in enumerate((gq_ref, gk_ref, gv_ref)):
        arrive(ref.at[:, :, col_part], c_recv.at[3 + n])
    for z in range(4):
        arrive(gw_last.at[z], g_recv.at[7 + z])
    gw_sumup[...] = (
        gw_last[0].astype(F32) + gw_last[1].astype(F32) + gw_last[2].astype(F32) + gw_last[3].astype(F32)
    ).astype(BF16)
    keep(gw_sumup, gw_ref, own_sem.at[8])
    arrive(col_in.at[:, pl.ds(0, 93)], c_send.at[0])
    arrive(col_out.at[0, pl.ds(0, 93)], c_send.at[1])
    arrive(col_gm.at[0, pl.ds(0, 93)], c_send.at[2])
    for n in range(3):
        arrive(col_out.at[n + 1, pl.ds(0, 93)], c_send.at[3 + n])
    arrive(col_out.at[0], c_send.at[6])
    for copy in local[4:]:
        copy.wait()
    for copy in sends:
        copy.wait_send()
    for other, copy in ends:

        @pl.when(other)
        def _():
            copy.wait_send()

    @pl.when(away)
    def _():
        w_away.wait_send()


def hand_over(*refs):
    sources, targets, buffers, in_sem, out_sem = refs[:5], refs[5:10], refs[10:15], refs[15], refs[16]
    loads = [pltpu.make_async_copy(sources[n], buffers[n], in_sem.at[n]) for n in range(5)]
    stores = [pltpu.make_async_copy(buffers[n], targets[n], out_sem.at[n]) for n in range(5)]
    for copy in loads:
        copy.start()
    for load, store in zip(loads, stores):
        load.wait()
        store.start()
    for copy in stores:
        copy.wait()


def per_device(query, key, value, weight_out, output_gradient):
    rows = jax.ShapeDtypeStruct((3, 256, 512), BF16)
    flat = jax.ShapeDtypeStruct((768, 512), BF16)
    any_space = pl.BlockSpec(memory_space=pl.ANY)
    dma = pltpu.SemaphoreType.DMA

    def half(*shape):
        return pltpu.VMEM(shape, BF16)

    def full(*shape):
        return pltpu.VMEM(shape, F32)

    results = pl.pallas_call(
        layer_kernel,
        out_shape=(rows, rows, rows, rows, jax.ShapeDtypeStruct((512, 128), BF16)),
        in_specs=[any_space] * 5,
        out_specs=(any_space,) * 5,
        scratch_shapes=[
            half(2, 512, 2048),
            half(768, 2048),
            half(3, 256, 256),
            half(4, 256, 256),
            half(4, 256, 256),
            half(3, 2, 256, 256),
            half(3, 256, 512),
            half(3, 256, 512),
            half(3, 256, 256),
            half(3, 256, 256),
            half(3, 256, 512),
            half(3, 256, 512),
            full(4, 256, 256),
            full(4, 256, 256),
            half(2, 256, 256),
            half(2, 256, 256),
            half(3, 96, 16, 128),
            half(2, 96, 16, 128),
            half(4, 96, 16, 128),
            full(5, 1552, 128),
            half(16, 96, 96),
            half(768, 2048),
            half(384, 512),
            half(384, 512),
            half(768, 512),
            half(768, 512),
            full(3, 256, 512),
            half(3, 3, 256, 256),
            half(3, 256, 512),
            half(512, 128),
            half(2, 4, 2, 2, 512, 128),
            half(4, 2, 2, 512, 128),
            half(4, 2, 2, 512, 128),
            half(3, 2, 2, 512, 128),
            half(2, 2, 512, 128),
            half(4, 512, 128),
            dma((9,)),
            dma((18,)),
            dma((18,)),
            dma((6,)),
            dma((6,)),
            dma((3,)),
            dma((3,)),
            dma((8,)),
            dma((8,)),
            dma((6,)),
            dma((6,)),
            dma((2,)),
            dma((2,)),
            dma((11,)),
            dma((11,)),
        ],
        compiler_params=pltpu.CompilerParams(
            collective_id=0, has_side_effects=True, vmem_limit_bytes=62 * 2**20
        ),
    )(
        query.reshape(3, 256, 512),
        key.reshape(3, 256, 512),
        value.reshape(3, 256, 512),
        weight_out,
        output_gradient,
    )
    return pl.pallas_call(
        hand_over,
        out_shape=(flat, flat, flat, flat, jax.ShapeDtypeStruct((512, 128), BF16)),
        in_specs=[any_space] * 5,
        out_specs=(any_space,) * 5,
        scratch_shapes=[half(768, 512)] * 4 + [half(512, 128), dma((5,)), dma((5,))],
    )(*(array.reshape(-1, array.shape[-1]) for array in results))


def solution(mesh):
    in_specs = (P("seq", "mp"), P("seq", "mp"), P("seq", "mp"), P("mp", "seq"), P("seq", "mp"))
    out_specs = (P("seq", "mp"), P("seq", "mp"), P("seq", "mp"), P("seq", "mp"), P("mp", "seq"))
    return jax.shard_map(
        per_device, mesh=mesh, in_specs=in_specs, out_specs=out_specs, check_vma=False
    )
```
